32 devices in a mesh: dp: 4 (over y, x), pipe: 2 (over core), seq: 4 (over z).
Axes of the slice: x: 2, y: 2, z: 4, core: 2. Of those that a mesh axis runs over, the one named last changes fastest.
Arguments:
- query_first: bfloat16 [4, 2, 256, 4096], P('dp', 'pipe', 'seq'), may hold values from -5 to 5
- key_first: bfloat16 [4, 2, 256, 512], P('dp', 'pipe', 'seq'), may hold values from -5 to 5
- value_first: bfloat16 [4, 2, 256, 512], P('dp', 'pipe', 'seq'), may hold values from -36 to 36
- query_second: bfloat16 [4, 2, 256, 4096], P('dp', 'pipe', 'seq'), may hold values from -5 to 5
- key_second: bfloat16 [4, 2, 256, 512], P('dp', 'pipe', 'seq'), may hold values from -5 to 5
- value_second: bfloat16 [4, 2, 256, 512], P('dp', 'pipe', 'seq'), may hold values from -36 to 36
- grad_output: bfloat16 [4, 2, 256, 4096], P('dp', 'pipe', 'seq'), may hold values from -6 to 6
- gain: bfloat16 [2, 4096], P('pipe'), may hold values from 0.5 to 1.5
Outputs:
- next_input: bfloat16 [4, 2, 256, 4096], P('dp', 'pipe', 'seq')
- grad_query: bfloat16 [4, 2, 256, 4096], P('dp', 'pipe', 'seq')
- grad_key: bfloat16 [4, 2, 256, 512], P('dp', 'pipe', 'seq')
- grad_value: bfloat16 [4, 2, 256, 512], P('dp', 'pipe', 'seq')
- grad_gain: float32 [2, 4096], P('pipe', 'seq')
The draws below stay inside these ranges and needn't reach their ends.
All inputs are finite; a program needn't handle non-finite values.
Results may differ from the reference program's by a relative error of at most 0.012.
The reference program's roundings to bfloat16 on the way count: a program that leaves them out, or rounds other values in their place, can miss the bound.
Values may be sent and summed in bfloat16 or wider, within the bound.
A program may use at most 64 MiB of HBM per device.

```python
import math
import jax
import jax.numpy as jnp
from jax import lax

SEQ_LEN = 256
QH = 32
KVH = 4
HD = 128
REPLICAS = 4
SECTIONS = 2


def drawn_pair(key, salt):
    key = jax.random.fold_in(key, salt)
    query_seed, keys_seed = jax.random.split(key, 2)
    query = jnp.clip(jax.random.normal(query_seed, (REPLICAS, SECTIONS, SEQ_LEN, QH, HD), jnp.float32), -4.0, 4.0)
    keys = jnp.clip(jax.random.normal(keys_seed, (REPLICAS, SECTIONS, SEQ_LEN, KVH, HD), jnp.float32), -4.0, 4.0)
    return (query.reshape(REPLICAS, SECTIONS, SEQ_LEN, QH * HD), keys.reshape(REPLICAS, SECTIONS, SEQ_LEN, KVH * HD))


def scaled_values(key):
    base = jnp.clip(jax.random.normal(key, (REPLICAS, SECTIONS, SEQ_LEN, KVH, HD), jnp.float32), -4.0, 4.0)
    scales = 3.0 ** (jnp.arange(KVH, dtype=jnp.float32) / max(KVH - 1, 1))
    return (base * scales[:, None]).reshape(REPLICAS, SECTIONS, SEQ_LEN, KVH * HD)


def draw_query_first(key, part):
    query, keys = drawn_pair(key, 11)
    return query.astype(jnp.bfloat16)


def draw_key_first(key, part):
    query, keys = drawn_pair(key, 11)
    return keys.astype(jnp.bfloat16)


def draw_query_second(key, part):
    query, keys = drawn_pair(key, 12)
    return query.astype(jnp.bfloat16)


def draw_key_second(key, part):
    query, keys = drawn_pair(key, 12)
    return keys.astype(jnp.bfloat16)


def draw_value_first(key, part):
    key = jax.random.fold_in(key, 21)
    return scaled_values(key).astype(jnp.bfloat16)


def draw_value_second(key, part):
    key = jax.random.fold_in(key, 22)
    return scaled_values(key).astype(jnp.bfloat16)


def level_of(own_key, dims, cuts, smallest, largest):
    loudness = 1.0
    for dim, blocks in cuts:
        heights = jax.random.uniform(jax.random.fold_in(jax.random.fold_in(own_key, 6), dim), (blocks,), jnp.float32, smallest / len(cuts), largest / len(cuts))
        loudness = loudness * jnp.repeat(jnp.exp(heights), dims[dim] // blocks).reshape((-1,) + (1,) * (len(dims) - 1 - dim))
    return loudness


def scatter_about(key, extent, width, bound, shards=(), kind=jnp.bfloat16):
    entries = width * jax.random.normal(key, extent, jnp.float32)
    if shards:
        entries = entries * level_of(key, extent, shards, -0.22, 0.18)
    return jnp.clip(entries, -bound, bound).astype(kind)


def setup_inputs(seed: int = 0) -> dict:
    streams_of = jax.random.split(jax.random.key(seed), 9)
    return {
        "query_first": draw_query_first(jax.random.fold_in(streams_of[8], 71), 0),
        "key_first": draw_key_first(jax.random.fold_in(streams_of[8], 71), 0),
        "value_first": draw_value_first(jax.random.fold_in(streams_of[8], 71), 0),
        "query_second": draw_query_second(jax.random.fold_in(streams_of[8], 71), 0),
        "key_second": draw_key_second(jax.random.fold_in(streams_of[8], 71), 0),
        "value_second": draw_value_second(jax.random.fold_in(streams_of[8], 71), 0),
        "grad_output": scatter_about(streams_of[6], (REPLICAS, SECTIONS, SEQ_LEN, QH * HD), 1.0, 6.0, ((0, 4), (1, 2), (2, 4))),
        "gain": jnp.clip(1.0 + 0.1 * jax.random.normal(streams_of[7], (SECTIONS, QH * HD), jnp.float32), 0.5, 1.5).astype(jnp.bfloat16),
    }


epsilon = 1e-05

def rounded(values):
    return lax.optimization_barrier(values.astype(jnp.bfloat16)).astype(jnp.float32)

def expand_heads(keys):
    length = keys.shape[0]
    grouped = keys.astype(jnp.float32).reshape(length, KVH, 1, HD)
    return jnp.broadcast_to(grouped, (length, KVH, QH // KVH, HD)).reshape(length, QH, HD)

def attention_probs(query, keys):
    length = query.shape[0]
    queries = query.astype(jnp.float32).reshape(length, QH, HD)
    scores = jnp.einsum('ihd,jhd->hij', queries, expand_heads(keys)) * (1.0 / math.sqrt(HD))
    positions = jnp.arange(length)
    allowed = positions[None, :] <= positions[:, None]
    scores = jnp.where(allowed[None], scores, -jnp.inf)
    exponent = jnp.exp(scores - lax.optimization_barrier(jnp.max(scores, axis=-1, keepdims=True)))
    return exponent / lax.optimization_barrier(jnp.sum(exponent, axis=-1, keepdims=True))

def attend(query, keys, values):
    length = query.shape[0]
    probs = attention_probs(query, keys)
    result = jnp.einsum('hij,jhd->ihd', rounded(probs), expand_heads(values))
    return result.reshape(length, QH * HD).astype(jnp.bfloat16)

def attend_backward(query, keys, values, output, grad_attn):
    length = query.shape[0]
    probs = attention_probs(query, keys)
    weights = rounded(probs)
    grad_heads = grad_attn.astype(jnp.float32).reshape(length, QH, HD)
    grad_value = jnp.einsum('hij,ihd->jhd', weights, grad_heads)
    grad_value = grad_value.reshape(length, KVH, QH // KVH, HD).sum(axis=2)
    grad_weights = jnp.einsum('ihd,jhd->hij', grad_heads, expand_heads(values))
    row_dots = lax.optimization_barrier(jnp.sum(grad_heads * output.astype(jnp.float32).reshape(length, QH, HD), axis=-1))
    grad_scores = rounded(probs * (grad_weights - row_dots.T[:, :, None]) * (1.0 / math.sqrt(HD)))
    grad_query = jnp.einsum('hij,jhd->ihd', grad_scores, expand_heads(keys))
    queries = query.astype(jnp.float32).reshape(length, QH, HD)
    grad_key = jnp.einsum('hij,ihd->jhd', grad_scores, queries)
    grad_key = grad_key.reshape(length, KVH, QH // KVH, HD).sum(axis=2)
    return (grad_query.reshape(length, QH * HD).astype(jnp.bfloat16), grad_key.reshape(length, KVH * HD).astype(jnp.bfloat16), grad_value.reshape(length, KVH * HD).astype(jnp.bfloat16))

def section_step(inputs):
    first_query, first_keys, first_values, second_query, second_keys, second_values, upstream, gain_row = inputs
    gain_float = gain_row.astype(jnp.float32)
    first_out = attend(first_query, first_keys, first_values).astype(jnp.float32)
    first_inverse = lax.rsqrt(lax.optimization_barrier(jnp.mean(first_out * first_out, axis=-1, keepdims=True)) + epsilon)
    normed = (gain_float * first_out * first_inverse).astype(jnp.bfloat16)
    second_out = attend(second_query, second_keys, second_values)
    activity = second_out.astype(jnp.float32)
    inverse = lax.rsqrt(lax.optimization_barrier(jnp.mean(activity * activity, axis=-1, keepdims=True)) + epsilon)
    upstream_float = upstream.astype(jnp.float32)
    gained = gain_float * upstream_float
    cross_mean = lax.optimization_barrier(jnp.mean(gained * activity, axis=-1, keepdims=True))
    grad_attn = (gained * inverse - activity * inverse ** 3 * cross_mean).astype(jnp.bfloat16)
    grad_gain = lax.optimization_barrier(jnp.sum(upstream_float * activity * inverse, axis=0))
    grad_query, grad_key, grad_value = attend_backward(second_query, second_keys, second_values, second_out, grad_attn)
    return (normed, grad_query, grad_key, grad_value, grad_gain)

def reference(query_first, key_first, value_first, query_second, key_second, value_second, grad_output, gain):
    replicas = query_first.shape[0]
    sections = query_first.shape[1]
    upstream = jnp.roll(grad_output, -1, axis=1)
    gains = jnp.broadcast_to(gain[None], (replicas,) + gain.shape)

    def flatten(array):
        return array.reshape((replicas * sections,) + array.shape[2:])

    def unflatten(array):
        return array.reshape((replicas, sections) + array.shape[1:])
    inputs = tuple((flatten(array) for array in (query_first, key_first, value_first, query_second, key_second, value_second, upstream, gains)))
    results = lax.map(section_step, inputs)
    normed, grad_query, grad_key, grad_value, grad_gain = [unflatten(array) for array in results]
    return (jnp.roll(normed, 1, axis=1), grad_query, grad_key, grad_value, lax.optimization_barrier(jnp.sum(grad_gain, axis=0)))
```

```python
import functools
import math

import jax
import jax.numpy as jnp
from jax import lax
from jax.experimental import pallas as pl
from jax.experimental.pallas import tpu as pltpu
from jax.sharding import PartitionSpec as P

QH = 32
KVH = 4
HD = 128
HPG = QH // KVH
WIDTH = QH * HD
EPS = 1e-05
SCALE = 1.0 / math.sqrt(HD)
SCALE_LOG2 = SCALE * math.log2(math.e)
MESH = pl.DeviceIdType.MESH
F32 = jnp.float32
BF16 = jnp.bfloat16


def head(h):
    return slice(h * HD, (h + 1) * HD)


def dot(a, b, contract):
    return lax.dot_general(a, b, ((contract[:1], contract[1:]), ((), ())), preferred_element_type=F32)


def kernel(
    n, pipes, replicas, rows,
    q1_in, k1_in, v1_in, q2_in, k2_in, v2_in, go_in, gain_ref,
    next_out, gq_out, gk_out, gv_out, gain_out,
    q1, q2, up, k1, v1, k2, v2, probs, o1, o2, grad, gq, part, own, land,
    gpart, gland, gshare,
    local_sem, kv_send, kv_recv, part_send, part_recv, out_sem,
    pipe_send, pipe_recv, gain_send, gain_recv, rep_send, rep_recv,
):
    me = lax.axis_index("seq")
    section = lax.axis_index("pipe")
    replica = lax.axis_index("dp")
    length = n * rows
    behind = lax.rem(section + pipes - 1, pipes)
    ahead = lax.rem(section + 1, pipes)

    def block(b):
        return pl.ds(pl.multiple_of(b * rows, rows), rows)

    locals_ = [
        pltpu.make_async_copy(src, dst, local_sem.at[i])
        for i, (src, dst) in enumerate(
            (
                (q2_in, q2),
                (k2_in, k2.at[block(me)]),
                (v2_in, v2.at[block(me)]),
                (q1_in, q1),
                (k1_in, k1.at[block(me)]),
                (v1_in, v1.at[block(me)]),
            )
        )
    ]
    for copy in locals_:
        copy.start()

    barrier = pltpu.get_barrier_semaphore()
    for d in range(1, n):
        pl.semaphore_signal(barrier, inc=1, device_id={"seq": lax.rem(me + d, n)}, device_id_type=MESH)
    for d in range(1, replicas):
        pl.semaphore_signal(
            barrier, inc=1, device_id={"dp": lax.rem(replica + d, replicas)}, device_id_type=MESH
        )
    for other in (behind, ahead):
        pl.semaphore_signal(barrier, inc=1, device_id={"pipe": other}, device_id_type=MESH)

    for b in range(1, n):

        @pl.when(b > me)
        def _():
            for ref in (k1, v1, k2, v2):
                ref[b * rows : (b + 1) * rows, :] = jnp.zeros((rows, KVH * HD), BF16)

    pl.semaphore_wait(barrier, n - 1 + replicas - 1 + 2)

    def kv_copy(array, g, d, source):
        src = (k2_in, v2_in, k1_in, v1_in)[array]
        dst = (k2, v2, k1, v1)[array]
        return pltpu.make_async_remote_copy(
            src_ref=src.at[:, head(g)],
            dst_ref=dst.at[block(source), head(g)],
            send_sem=kv_send.at[array, g, d - 1],
            recv_sem=kv_recv.at[array, g, d - 1],
            device_id={"seq": lax.rem(me + d, n)},
            device_id_type=MESH,
        )

    def kv_start(arrays, g):
        for d in range(n - 1, 0, -1):

            @pl.when(me + d < n)
            def _():
                for array in arrays:
                    kv_copy(array, g, d, me).start()

    def kv_wait(arrays, g):
        for d in range(1, n):

            @pl.when(me >= d)
            def _():
                for array in arrays:
                    kv_copy(array, g, d, me - d).wait_recv()

    for g in range(KVH):
        kv_start((0, 1), g)
    upstream = pltpu.make_async_remote_copy(
        src_ref=go_in, dst_ref=up, send_sem=pipe_send.at[0], recv_sem=pipe_recv.at[0],
        device_id={"pipe": behind}, device_id_type=MESH,
    )
    upstream.start()
    for g in range(KVH):
        kv_start((2, 3), g)

    token = me * rows + lax.broadcasted_iota(jnp.int32, (rows, length), 0)
    allowed = (lax.broadcasted_iota(jnp.int32, (rows, length), 1) <= token)[None]

    def stack(ref, g):
        return jnp.concatenate([ref[:, head(g * HPG + h)] for h in range(HPG)], axis=0)

    def forward(q, k, v, o, g):
        scores = dot(stack(q, g), k[:, head(g)], (1, 1)).reshape(HPG, rows, length)
        scores = jnp.where(allowed, scores, -jnp.inf)
        highest = jnp.max(scores, axis=-1, keepdims=True)
        exponent = jnp.exp2((scores - highest) * SCALE_LOG2)
        prob = exponent * (1.0 / jnp.sum(exponent, axis=-1, keepdims=True))
        prob = prob.reshape(HPG * rows, length)
        out = dot(prob.astype(BF16), v[:, head(g)], (1, 0)).astype(BF16)
        squares = jnp.zeros((rows, HD), F32)
        for h in range(HPG):
            piece = out[h * rows : (h + 1) * rows]
            o[:, head(g * HPG + h)] = piece
            squares += piece.astype(F32) * piece.astype(F32)
        return prob, squares

    def inverse_of(squares):
        return lax.rsqrt(jnp.sum(squares, axis=-1, keepdims=True) * (1.0 / WIDTH) + EPS)

    for copy in locals_[:3]:
        copy.wait()
    squares = jnp.zeros((rows, HD), F32)
    for g in range(KVH):
        kv_wait((0, 1), g)
        prob, more = forward(q2, k2, v2, o2, g)
        probs[g] = prob
        squares += more
    inverse = inverse_of(squares)

    upstream.wait_recv()
    cross = jnp.zeros((rows, HD), F32)
    share = QH // n
    for h in range(QH):
        activity = o2[:, head(h)].astype(F32)
        product = up[:, head(h)].astype(F32) * activity
        cross += gain_ref[:, head(h)].astype(F32) * product
        gpart[h // share, h % share : h % share + 1, :] = jnp.sum(product * inverse, axis=0, keepdims=True)
    cross_mean = jnp.sum(cross, axis=-1, keepdims=True) * (1.0 / WIDTH)
    factor = inverse * inverse * inverse * cross_mean
    for h in range(QH):
        gained = gain_ref[:, head(h)].astype(F32) * up[:, head(h)].astype(F32)
        grad[:, head(h)] = (gained * inverse - o2[:, head(h)].astype(F32) * factor).astype(BF16)

    def gain_copy(d):
        owner = lax.rem(me + d, n)
        return pltpu.make_async_remote_copy(
            src_ref=gpart.at[owner], dst_ref=gland.at[d - 1],
            send_sem=gain_send.at[d - 1], recv_sem=gain_recv.at[d - 1],
            device_id={"seq": owner}, device_id_type=MESH,
        )

    for d in range(1, n):
        gain_copy(d).start()

    def part_copy(g, d, target):
        return pltpu.make_async_remote_copy(
            src_ref=part.at[target, g], dst_ref=land.at[d - 1, g],
            send_sem=part_send.at[g, d - 1], recv_sem=part_recv.at[g, d - 1],
            device_id={"seq": target}, device_id_type=MESH,
        )

    def gq_copy(g):
        lanes = slice(g * HPG * HD, (g + 1) * HPG * HD)
        return pltpu.make_async_copy(gq.at[:, lanes], gq_out.at[:, lanes], out_sem.at[g])

    for g in range(KVH):
        grads = stack(grad, g)
        outs = stack(o2, g)
        prob = probs[g]
        dots = jnp.sum(grads.astype(F32) * outs.astype(F32), axis=-1, keepdims=True)
        grad_weights = dot(grads, v2[:, head(g)], (1, 1))
        grad_scores = (prob * (grad_weights - dots) * SCALE).astype(BF16)
        for which, value in enumerate(
            (dot(grad_scores, stack(q2, g), (0, 0)), dot(prob.astype(BF16), grads, (0, 0)))
        ):
            own[g, which] = value
            for b in range(n - 1):
                part[b, g, which] = value[b * rows : (b + 1) * rows].astype(BF16)
        for d in range(n - 1, 0, -1):

            @pl.when(me >= d)
            def _():
                part_copy(g, d, me - d).start()

        grad_query = dot(grad_scores, k2[:, head(g)], (1, 0)).astype(BF16)
        for h in range(HPG):
            gq[:, head(g * HPG + h)] = grad_query[h * rows : (h + 1) * rows]
        gq_copy(g).start()

    for d in range(1, n):
        gain_copy(d).wait_recv()
    total = gpart[me]
    for d in range(1, n):
        total += gland[d - 1]
    gshare[replica] = total

    def replica_copy(d, source):
        return pltpu.make_async_remote_copy(
            src_ref=gshare.at[source], dst_ref=gshare.at[source],
            send_sem=rep_send.at[d - 1], recv_sem=rep_recv.at[d - 1],
            device_id={"dp": lax.rem(replica + d, replicas)}, device_id_type=MESH,
        )

    for d in range(1, replicas):
        replica_copy(d, replica).start()

    for copy in locals_[3:]:
        copy.wait()
    squares = jnp.zeros((rows, HD), F32)
    for g in range(KVH):
        kv_wait((2, 3), g)
        prob, more = forward(q1, k1, v1, o1, g)
        squares += more
    inverse = inverse_of(squares)
    for h in range(QH):
        gain = gain_ref[:, head(h)].astype(F32)
        o1[:, head(h)] = (gain * o1[:, head(h)].astype(F32) * inverse).astype(BF16)
    normed = pltpu.make_async_remote_copy(
        src_ref=o1, dst_ref=next_out, send_sem=pipe_send.at[1], recv_sem=pipe_recv.at[1],
        device_id={"pipe": ahead}, device_id_type=MESH,
    )
    normed.start()

    for g in range(KVH):
        for d in range(1, n):

            @pl.when(me + d < n)
            def _():
                part_copy(g, d, me).wait_recv()
                for which in range(2):
                    own[g, which, block(me), :] += land[d - 1, g, which].astype(F32)

        gk_out[:, head(g)] = own[g, 0, block(me), :].astype(BF16)
        gv_out[:, head(g)] = own[g, 1, block(me), :].astype(BF16)

    for d in range(1, replicas):
        replica_copy(d, lax.rem(replica + replicas - d, replicas)).wait_recv()
    total = gshare[0]
    for r in range(1, replicas):
        total += gshare[r]
    for h in range(share):
        gain_out[:, head(h)] = total[h : h + 1]

    for d in range(1, n):

        @pl.when(me + d < n)
        def _():
            for g in range(KVH):
                for array in range(4):
                    kv_copy(array, g, d, me).wait_send()

        @pl.when(me >= d)
        def _():
            for g in range(KVH):
                part_copy(g, d, me - d).wait_send()

        gain_copy(d).wait_send()
    for d in range(1, replicas):
        replica_copy(d, replica).wait_send()
    upstream.wait_send()
    for g in range(KVH):
        gq_copy(g).wait()
    normed.wait()


def local(n, pipes, replicas, q1, k1, v1, q2, k2, v2, go, gain):
    rows = q1.shape[2]
    length = n * rows
    share = QH // n
    args = [x[0, 0] for x in (q1, k1, v1, q2, k2, v2, go)] + [gain]
    anywhere = pl.BlockSpec(memory_space=pl.ANY)
    vmem = pl.BlockSpec(memory_space=pltpu.VMEM)
    wide = pltpu.VMEM((rows, WIDTH), BF16)
    keys = pltpu.VMEM((length, KVH * HD), BF16)
    dma = pltpu.SemaphoreType.DMA
    flops = 2 * 7 * rows * length * HD * QH
    outs = pl.pallas_call(
        functools.partial(kernel, n, pipes, replicas, rows),
        out_shape=(
            jax.ShapeDtypeStruct((rows, WIDTH), BF16),
            jax.ShapeDtypeStruct((rows, WIDTH), BF16),
            jax.ShapeDtypeStruct((rows, KVH * HD), BF16),
            jax.ShapeDtypeStruct((rows, KVH * HD), BF16),
            jax.ShapeDtypeStruct((1, WIDTH // n), F32),
        ),
        in_specs=[anywhere] * 7 + [vmem],
        out_specs=(anywhere, anywhere, vmem, vmem, vmem),
        scratch_shapes=[
            wide, wide, wide, keys, keys, keys, keys,
            pltpu.VMEM((KVH, HPG * rows, length), F32),
            wide, wide, wide, wide,
            pltpu.VMEM((n, KVH, 2, rows, HD), BF16),
            pltpu.VMEM((KVH, 2, length, HD), F32),
            pltpu.VMEM((n - 1, KVH, 2, rows, HD), BF16),
            pltpu.VMEM((n, share, HD), F32),
            pltpu.VMEM((n - 1, share, HD), F32),
            pltpu.VMEM((replicas, share, HD), F32),
            dma((6,)),
            dma((4, KVH, n - 1)), dma((4, KVH, n - 1)),
            dma((KVH, n - 1)), dma((KVH, n - 1)),
            dma((KVH,)),
            dma((2,)), dma((2,)),
            dma((n - 1,)), dma((n - 1,)),
            dma((replicas - 1,)), dma((replicas - 1,)),
        ],
        compiler_params=pltpu.CompilerParams(
            collective_id=0, has_side_effects=True, vmem_limit_bytes=48 * 1024 * 1024
        ),
        cost_estimate=pl.CostEstimate(flops=flops, bytes_accessed=8 * rows * WIDTH, transcendentals=0),
    )(*args)
    nxt, gq, gk, gv, gg = outs
    return nxt[None, None], gq[None, None], gk[None, None], gv[None, None], gg


def solution(mesh):
    tokens = P("dp", "pipe", "seq", None)
    sizes = (mesh.shape["seq"], mesh.shape["pipe"], mesh.shape["dp"])
    return jax.shard_map(
        functools.partial(local, *sizes),
        mesh=mesh,
        in_specs=(tokens,) * 7 + (P("pipe", None),),
        out_specs=(tokens,) * 4 + (P("pipe", "seq"),),
        check_vma=False,
    )
```

```python
import functools
import math

import jax
import jax.numpy as jnp
from jax import lax
from jax.experimental import pallas as pl
from jax.experimental.pallas import tpu as pltpu
from jax.sharding import PartitionSpec as P

QH = 32
KVH = 4
HD = 128
HPG = QH // KVH
WIDTH = QH * HD
EPS = 1e-05
SCALE = 1.0 / math.sqrt(HD)
SCALE_LOG2 = SCALE * math.log2(math.e)
VMEM_LIMIT = 60 * 1024 * 1024
MESH = pl.DeviceIdType.MESH
F32 = jnp.float32
BF16 = jnp.bfloat16


def head(h):
    return slice(h * HD, (h + 1) * HD)


def dot(a, b, contract):
    return lax.dot_general(a, b, ((contract[:1], contract[1:]), ((), ())), preferred_element_type=F32)


def kernel(
    n, pipes, replicas, rows,
    q1_in, k1_in, v1_in, q2_in, k2_in, v2_in, go_in, gain_in,
    next_out, gq_out, gk_out, gv_out, gain_out,
    gain_ref, q1, q2, up, k1, v1, k2, v2, probs, o1, o2, grad, gq, part, own, land,
    gpart, gland, gshare,
    local_sem, kv_send, kv_recv, part_send, part_recv, out_sem,
    pipe_send, pipe_recv, gain_send, gain_recv, rep_send, rep_recv,
):
    me = lax.axis_index("seq")
    section = lax.axis_index("pipe")
    replica = lax.axis_index("dp")
    length = n * rows
    behind = lax.rem(section + pipes - 1, pipes)
    ahead = lax.rem(section + 1, pipes)

    def block(b):
        return pl.ds(pl.multiple_of(b * rows, rows), rows)

    locals_ = [
        pltpu.make_async_copy(src, dst, local_sem.at[i])
        for i, (src, dst) in enumerate(
            (
                (q2_in, q2),
                (k2_in, k2.at[block(me)]),
                (v2_in, v2.at[block(me)]),
                (gain_in, gain_ref),
                (q1_in, q1),
                (k1_in, k1.at[block(me)]),
                (v1_in, v1.at[block(me)]),
            )
        )
    ]
    for copy in locals_:
        copy.start()

    barrier = pltpu.get_barrier_semaphore()
    for d in range(1, n):
        pl.semaphore_signal(barrier, inc=1, device_id={"seq": lax.rem(me + d, n)}, device_id_type=MESH)
    for d in range(1, replicas):
        pl.semaphore_signal(
            barrier, inc=1, device_id={"dp": lax.rem(replica + d, replicas)}, device_id_type=MESH
        )
    for other in (behind, ahead):
        pl.semaphore_signal(barrier, inc=1, device_id={"pipe": other}, device_id_type=MESH)

    for b in range(1, n):

        @pl.when(b > me)
        def _():
            for ref in (k1, v1, k2, v2):
                ref[b * rows : (b + 1) * rows, :] = jnp.zeros((rows, KVH * HD), BF16)

    pl.semaphore_wait(barrier, n - 1 + replicas - 1 + 2)

    def kv_copy(array, g, d, source):
        src = (k2_in, v2_in, k1_in, v1_in)[array]
        dst = (k2, v2, k1, v1)[array]
        return pltpu.make_async_remote_copy(
            src_ref=src.at[:, head(g)],
            dst_ref=dst.at[block(source), head(g)],
            send_sem=kv_send.at[array, g, d - 1],
            recv_sem=kv_recv.at[array, g, d - 1],
            device_id={"seq": lax.rem(me + d, n)},
            device_id_type=MESH,
        )

    def kv_start(arrays, g):
        for d in range(n - 1, 0, -1):

            @pl.when(me + d < n)
            def _():
                for array in arrays:
                    kv_copy(array, g, d, me).start()

    def kv_wait(arrays, g):
        for d in range(1, n):

            @pl.when(me >= d)
            def _():
                for array in arrays:
                    kv_copy(array, g, d, me - d).wait_recv()

    for g in range(KVH):
        kv_start((0, 1), g)
    upstream = pltpu.make_async_remote_copy(
        src_ref=go_in, dst_ref=up, send_sem=pipe_send.at[0], recv_sem=pipe_recv.at[0],
        device_id={"pipe": behind}, device_id_type=MESH,
    )
    upstream.start()
    for g in range(KVH):
        kv_start((2, 3), g)

    token = me * rows + lax.broadcasted_iota(jnp.int32, (rows, length), 0)
    allowed = (lax.broadcasted_iota(jnp.int32, (rows, length), 1) <= token)[None]

    def stack(ref, g):
        return jnp.concatenate([ref[:, head(g * HPG + h)] for h in range(HPG)], axis=0)

    def forward(q, k, v, o, g):
        scores = dot(stack(q, g), k[:, head(g)], (1, 1)).reshape(HPG, rows, length)
        scores = jnp.where(allowed, scores, -jnp.inf)
        highest = jnp.max(scores, axis=-1, keepdims=True)
        exponent = jnp.exp2((scores - highest) * SCALE_LOG2)
        prob = exponent * (1.0 / jnp.sum(exponent, axis=-1, keepdims=True))
        prob = prob.reshape(HPG * rows, length)
        out = dot(prob.astype(BF16), v[:, head(g)], (1, 0)).astype(BF16)
        squares = jnp.zeros((rows, HD), F32)
        for h in range(HPG):
            piece = out[h * rows : (h + 1) * rows]
            o[:, head(g * HPG + h)] = piece
            squares += piece.astype(F32) * piece.astype(F32)
        return prob, squares

    def inverse_of(squares):
        return lax.rsqrt(jnp.sum(squares, axis=-1, keepdims=True) * (1.0 / WIDTH) + EPS)

    for copy in locals_[:4]:
        copy.wait()
    squares = jnp.zeros((rows, HD), F32)
    for g in range(KVH):
        kv_wait((0, 1), g)
        prob, more = forward(q2, k2, v2, o2, g)
        probs[g] = prob
        squares += more
    inverse = inverse_of(squares)

    upstream.wait_recv()
    cross = jnp.zeros((rows, HD), F32)
    share = QH // n
    for h in range(QH):
        activity = o2[:, head(h)].astype(F32)
        product = up[:, head(h)].astype(F32) * activity
        cross += gain_ref[:, head(h)].astype(F32) * product
        gpart[h // share, h % share : h % share + 1, :] = jnp.sum(product * inverse, axis=0, keepdims=True)
    cross_mean = jnp.sum(cross, axis=-1, keepdims=True) * (1.0 / WIDTH)
    factor = inverse * inverse * inverse * cross_mean
    for h in range(QH):
        gained = gain_ref[:, head(h)].astype(F32) * up[:, head(h)].astype(F32)
        grad[:, head(h)] = (gained * inverse - o2[:, head(h)].astype(F32) * factor).astype(BF16)

    def gain_copy(d):
        owner = lax.rem(me + d, n)
        return pltpu.make_async_remote_copy(
            src_ref=gpart.at[owner], dst_ref=gland.at[d - 1],
            send_sem=gain_send.at[d - 1], recv_sem=gain_recv.at[d - 1],
            device_id={"seq": owner}, device_id_type=MESH,
        )

    for d in range(1, n):
        gain_copy(d).start()

    def part_copy(g, d, target):
        return pltpu.make_async_remote_copy(
            src_ref=part.at[target, g], dst_ref=land.at[d - 1, g],
            send_sem=part_send.at[g, d - 1], recv_sem=part_recv.at[g, d - 1],
            device_id={"seq": target}, device_id_type=MESH,
        )

    def gq_copy(g):
        lanes = slice(g * HPG * HD, (g + 1) * HPG * HD)
        return pltpu.make_async_copy(gq.at[:, lanes], gq_out.at[:, lanes], out_sem.at[g])

    for g in range(KVH):
        grads = stack(grad, g)
        outs = stack(o2, g)
        prob = probs[g]
        dots = jnp.sum(grads.astype(F32) * outs.astype(F32), axis=-1, keepdims=True)
        grad_weights = dot(grads, v2[:, head(g)], (1, 1))
        grad_scores = (prob * (grad_weights - dots) * SCALE).astype(BF16)
        for which, value in enumerate(
            (dot(grad_scores, stack(q2, g), (0, 0)), dot(prob.astype(BF16), grads, (0, 0)))
        ):
            own[g, which] = value
            for b in range(n - 1):
                part[b, g, which] = value[b * rows : (b + 1) * rows].astype(BF16)
        for d in range(n - 1, 0, -1):

            @pl.when(me >= d)
            def _():
                part_copy(g, d, me - d).start()

        grad_query = dot(grad_scores, k2[:, head(g)], (1, 0)).astype(BF16)
        for h in range(HPG):
            gq[:, head(g * HPG + h)] = grad_query[h * rows : (h + 1) * rows]
        gq_copy(g).start()

    for d in range(1, n):
        gain_copy(d).wait_recv()
    total = gpart[me]
    for d in range(1, n):
        total += gland[d - 1]
    gshare[replica] = total

    def replica_copy(d, source):
        return pltpu.make_async_remote_copy(
            src_ref=gshare.at[source], dst_ref=gshare.at[source],
            send_sem=rep_send.at[d - 1], recv_sem=rep_recv.at[d - 1],
            device_id={"dp": lax.rem(replica + d, replicas)}, device_id_type=MESH,
        )

    for d in range(1, replicas):
        replica_copy(d, replica).start()

    for copy in locals_[4:]:
        copy.wait()
    squares = jnp.zeros((rows, HD), F32)
    for g in range(KVH):
        kv_wait((2, 3), g)
        prob, more = forward(q1, k1, v1, o1, g)
        squares += more
    inverse = inverse_of(squares)
    for h in range(QH):
        gain = gain_ref[:, head(h)].astype(F32)
        o1[:, head(h)] = (gain * o1[:, head(h)].astype(F32) * inverse).astype(BF16)
    normed = pltpu.make_async_remote_copy(
        src_ref=o1, dst_ref=next_out, send_sem=pipe_send.at[1], recv_sem=pipe_recv.at[1],
        device_id={"pipe": ahead}, device_id_type=MESH,
    )
    normed.start()

    for g in range(KVH):
        for d in range(1, n):

            @pl.when(me + d < n)
            def _():
                part_copy(g, d, me).wait_recv()
                for which in range(2):
                    own[g, which, block(me), :] += land[d - 1, g, which].astype(F32)

        gk_out[:, head(g)] = own[g, 0, block(me), :].astype(BF16)
        gv_out[:, head(g)] = own[g, 1, block(me), :].astype(BF16)

    for d in range(1, replicas):
        replica_copy(d, lax.rem(replica + replicas - d, replicas)).wait_recv()
    total = gshare[0]
    for r in range(1, replicas):
        total += gshare[r]
    for h in range(share):
        gain_out[:, head(h)] = total[h : h + 1]

    for d in range(1, n):

        @pl.when(me + d < n)
        def _():
            for g in range(KVH):
                for array in range(4):
                    kv_copy(array, g, d, me).wait_send()

        @pl.when(me >= d)
        def _():
            for g in range(KVH):
                part_copy(g, d, me - d).wait_send()

        gain_copy(d).wait_send()
    for d in range(1, replicas):
        replica_copy(d, replica).wait_send()
    upstream.wait_send()
    for g in range(KVH):
        gq_copy(g).wait()
    normed.wait()


def write_out(nxt, gq, own, land, gshare, nxt_out, gq_out, gk_out, gv_out, gain_out, sems):
    copies = [
        pltpu.make_async_copy(nxt, nxt_out, sems.at[0]),
        pltpu.make_async_copy(gq, gq_out, sems.at[1]),
        pltpu.make_async_copy(own, gk_out, sems.at[2]),
        pltpu.make_async_copy(land, gv_out, sems.at[3]),
        pltpu.make_async_copy(gshare, gain_out, sems.at[4]),
    ]
    for copy in copies:
        copy.start()
    for copy in copies:
        copy.wait()


def local(n, pipes, replicas, q1, k1, v1, q2, k2, v2, go, gain):
    rows = q1.shape[2]
    length = n * rows
    share = QH // n
    args = [x[0, 0] for x in (q1, k1, v1, q2, k2, v2, go)] + [gain]
    anywhere = pl.BlockSpec(memory_space=pl.ANY)
    hbm = pl.BlockSpec(memory_space=pltpu.HBM)
    vmem = pl.BlockSpec(memory_space=pltpu.VMEM)
    wide = pltpu.VMEM((rows, WIDTH), BF16)
    keys = pltpu.VMEM((length, KVH * HD), BF16)
    dma = pltpu.SemaphoreType.DMA
    flops = 2 * 7 * rows * length * HD * QH
    outs = pl.pallas_call(
        functools.partial(kernel, n, pipes, replicas, rows),
        out_shape=(
            jax.ShapeDtypeStruct((rows, WIDTH), BF16),
            jax.ShapeDtypeStruct((rows, WIDTH), BF16),
            jax.ShapeDtypeStruct((rows, KVH * HD), BF16),
            jax.ShapeDtypeStruct((rows, KVH * HD), BF16),
            jax.ShapeDtypeStruct((1, WIDTH // n), F32),
        ),
        in_specs=[hbm] * 8,
        out_specs=(anywhere, anywhere, vmem, vmem, vmem),
        scratch_shapes=[
            pltpu.VMEM((1, WIDTH), BF16),
            wide, wide, wide, keys, keys, keys, keys,
            pltpu.VMEM((KVH, HPG * rows, length), F32),
            wide, wide, wide, wide,
            pltpu.VMEM((n, KVH, 2, rows, HD), BF16),
            pltpu.VMEM((KVH, 2, length, HD), F32),
            pltpu.VMEM((n - 1, KVH, 2, rows, HD), BF16),
            pltpu.VMEM((n, share, HD), F32),
            pltpu.VMEM((n - 1, share, HD), F32),
            pltpu.VMEM((replicas, share, HD), F32),
            dma((7,)),
            dma((4, KVH, n - 1)), dma((4, KVH, n - 1)),
            dma((KVH, n - 1)), dma((KVH, n - 1)),
            dma((KVH,)),
            dma((2,)), dma((2,)),
            dma((n - 1,)), dma((n - 1,)),
            dma((replicas - 1,)), dma((replicas - 1,)),
        ],
        compiler_params=pltpu.CompilerParams(
            collective_id=0, has_side_effects=True, vmem_limit_bytes=VMEM_LIMIT
        ),
        cost_estimate=pl.CostEstimate(flops=flops, bytes_accessed=8 * rows * WIDTH, transcendentals=0),
    )(*args)
    nxt, gq, gk, gv, gg = pl.pallas_call(
        write_out,
        out_shape=tuple(jax.ShapeDtypeStruct(x.shape, x.dtype) for x in outs),
        in_specs=[anywhere] * 5,
        out_specs=(hbm,) * 5,
        scratch_shapes=[dma((5,))],
        compiler_params=pltpu.CompilerParams(vmem_limit_bytes=VMEM_LIMIT),
    )(*outs)
    return nxt[None, None], gq[None, None], gk[None, None], gv[None, None], gg


def solution(mesh):
    tokens = P("dp", "pipe", "seq", None)
    sizes = (mesh.shape["seq"], mesh.shape["pipe"], mesh.shape["dp"])
    return jax.shard_map(
        functools.partial(local, *sizes),
        mesh=mesh,
        in_specs=(tokens,) * 7 + (P("pipe", None),),
        out_specs=(tokens,) * 4 + (P("pipe", "seq"),),
        check_vma=False,
    )
```

```python
import functools
import math

import jax
import jax.numpy as jnp
from jax import lax
from jax.experimental import pallas as pl
from jax.experimental.pallas import tpu as pltpu
from jax.sharding import PartitionSpec as P

QH = 32
KVH = 4
HD = 128
HPG = QH // KVH
WIDTH = QH * HD
EPS = 1e-05
SCALE = 1.0 / math.sqrt(HD)
SCALE_LOG2 = SCALE * math.log2(math.e)
VMEM_LIMIT = 60 * 1024 * 1024
MESH = pl.DeviceIdType.MESH
F32 = jnp.float32
BF16 = jnp.bfloat16


def head(h):
    return slice(h * HD, (h + 1) * HD)


def dot(a, b, contract):
    return lax.dot_general(a, b, ((contract[:1], contract[1:]), ((), ())), preferred_element_type=F32)


def kernel(
    n, pipes, replicas, rows,
    q1_in, k1_in, v1_in, q2_in, k2_in, v2_in, go_in, gain_in,
    next_out, gq_out, gk_out, gv_out, gain_out,
    gain_ref, q1, q2, up, k1, v1, k2, v2, probs, o1, o2, grad, gq, part, own, land,
    gpart, gland, gshare,
    local_sem, kv_send, kv_recv, part_send, part_recv, out_sem,
    pipe_send, pipe_recv, gain_send, gain_recv, rep_send, rep_recv,
):
    me = lax.axis_index("seq")
    section = lax.axis_index("pipe")
    replica = lax.axis_index("dp")
    length = n * rows
    behind = lax.rem(section + pipes - 1, pipes)
    ahead = lax.rem(section + 1, pipes)

    def block(b):
        return pl.ds(pl.multiple_of(b * rows, rows), rows)

    locals_ = [
        pltpu.make_async_copy(src, dst, local_sem.at[i])
        for i, (src, dst) in enumerate(
            (
                (q2_in, q2),
                (k2_in, k2.at[block(me)]),
                (v2_in, v2.at[block(me)]),
                (gain_in, gain_ref),
                (q1_in, q1),
                (k1_in, k1.at[block(me)]),
                (v1_in, v1.at[block(me)]),
            )
        )
    ]
    for copy in locals_:
        copy.start()

    barrier = pltpu.get_barrier_semaphore()
    for d in range(1, n):
        pl.semaphore_signal(barrier, inc=1, device_id={"seq": lax.rem(me + d, n)}, device_id_type=MESH)
    for d in range(1, replicas):
        pl.semaphore_signal(
            barrier, inc=1, device_id={"dp": lax.rem(replica + d, replicas)}, device_id_type=MESH
        )
    for other in (behind, ahead):
        pl.semaphore_signal(barrier, inc=1, device_id={"pipe": other}, device_id_type=MESH)

    for b in range(1, n):

        @pl.when(b > me)
        def _():
            for ref in (k1, v1, k2, v2):
                ref[b * rows : (b + 1) * rows, :] = jnp.zeros((rows, KVH * HD), BF16)

    pl.semaphore_wait(barrier, n - 1 + replicas - 1 + 2)

    def kv_copy(array, g, d, source):
        own_block = (k2_in, v2_in, k1_in, v1_in)[array]
        dst = (k2, v2, k1, v1)[array]
        lanes = head(g) if array < 2 else slice(0, KVH * HD)
        src = own_block.at[:, lanes] if d <= 2 else dst.at[block(source), lanes]
        return pltpu.make_async_remote_copy(
            src_ref=src,
            dst_ref=dst.at[block(source), lanes],
            send_sem=kv_send.at[array, g, d - 1],
            recv_sem=kv_recv.at[array, g, d - 1],
            device_id={"seq": lax.rem(me + (d if d <= 2 else 1), n)},
            device_id_type=MESH,
        )

    def kv_start(arrays, g):
        for d in range(min(2, n - 1), 0, -1):

            @pl.when(me + d < n)
            def _():
                for array in arrays:
                    kv_copy(array, g, d, me).start()

    def kv_forward(arrays, g):
        for d in range(2, n - 1):

            @pl.when(jnp.logical_and(me >= d, me + 1 < n))
            def _():
                for array in arrays:
                    kv_copy(array, g, d, me - d).wait_recv()
                    kv_copy(array, g, d + 1, me - d).start()

    def kv_wait(arrays, g):
        for d in range(1, n):
            waits = me >= d if d == 1 else me == n - 1

            @pl.when(waits)
            def _():
                for array in arrays:
                    kv_copy(array, g, d, me - d).wait_recv()

    for g in range(KVH):
        kv_start((0, 1), g)
    upstream = pltpu.make_async_remote_copy(
        src_ref=go_in, dst_ref=up, send_sem=pipe_send.at[0], recv_sem=pipe_recv.at[0],
        device_id={"pipe": behind}, device_id_type=MESH,
    )
    upstream.start()

    token = me * rows + lax.broadcasted_iota(jnp.int32, (rows, length), 0)
    allowed = (lax.broadcasted_iota(jnp.int32, (rows, length), 1) <= token)[None]

    def stack(ref, g):
        return jnp.concatenate([ref[:, head(g * HPG + h)] for h in range(HPG)], axis=0)

    def forward(q, k, v, o, g):
        scores = dot(stack(q, g), k[:, head(g)], (1, 1)).reshape(HPG, rows, length)
        scores = jnp.where(allowed, scores, -jnp.inf)
        highest = jnp.max(scores, axis=-1, keepdims=True)
        exponent = jnp.exp2((scores - highest) * SCALE_LOG2)
        prob = exponent * (1.0 / jnp.sum(exponent, axis=-1, keepdims=True))
        prob = prob.reshape(HPG * rows, length)
        out = dot(prob.astype(BF16), v[:, head(g)], (1, 0)).astype(BF16)
        squares = jnp.zeros((rows, HD), F32)
        for h in range(HPG):
            piece = out[h * rows : (h + 1) * rows]
            o[:, head(g * HPG + h)] = piece
            squares += piece.astype(F32) * piece.astype(F32)
        return prob, squares

    def inverse_of(squares):
        return lax.rsqrt(jnp.sum(squares, axis=-1, keepdims=True) * (1.0 / WIDTH) + EPS)

    for copy in locals_[:4]:
        copy.wait()
    squares = jnp.zeros((rows, HD), F32)
    kv_forward((0, 1), 0)
    for g in range(KVH):
        if g + 1 < KVH:
            kv_forward((0, 1), g + 1)
        if g + 2 == KVH:
            kv_start((2, 3), 0)
        kv_wait((0, 1), g)
        prob, more = forward(q2, k2, v2, o2, g)
        probs[g] = prob
        squares += more
    inverse = inverse_of(squares)

    upstream.wait_recv()
    cross = jnp.zeros((rows, HD), F32)
    share = QH // n
    for h in range(QH):
        activity = o2[:, head(h)].astype(F32)
        product = up[:, head(h)].astype(F32) * activity
        cross += gain_ref[:, head(h)].astype(F32) * product
        gpart[h // share, h % share : h % share + 1, :] = jnp.sum(product * inverse, axis=0, keepdims=True)
    cross_mean = jnp.sum(cross, axis=-1, keepdims=True) * (1.0 / WIDTH)
    factor = inverse * inverse * inverse * cross_mean
    for h in range(QH):
        gained = gain_ref[:, head(h)].astype(F32) * up[:, head(h)].astype(F32)
        grad[:, head(h)] = (gained * inverse - o2[:, head(h)].astype(F32) * factor).astype(BF16)

    def gain_copy(d):
        owner = lax.rem(me + d, n)
        return pltpu.make_async_remote_copy(
            src_ref=gpart.at[owner], dst_ref=gland.at[d - 1],
            send_sem=gain_send.at[d - 1], recv_sem=gain_recv.at[d - 1],
            device_id={"seq": owner}, device_id_type=MESH,
        )

    for d in range(1, n):
        gain_copy(d).start()

    def part_copy(g, d, target):
        return pltpu.make_async_remote_copy(
            src_ref=part.at[target, g], dst_ref=land.at[d - 1, g],
            send_sem=part_send.at[g, d - 1], recv_sem=part_recv.at[g, d - 1],
            device_id={"seq": lax.rem(me + n - (d if d <= 2 else 1), n)}, device_id_type=MESH,
        )

    def part_relay(g):
        for d in range(n - 2, 1, -1):

            @pl.when(jnp.logical_and(me >= d, me + 1 < n))
            def _():
                target = me - d
                part_copy(g, d + 1, target).wait_recv()
                for which in range(2):
                    total = own[g, which, block(target), :] + land[d, g, which].astype(F32)
                    part[target, g, which] = total.astype(BF16)
                part_copy(g, d, target).start()

    def gq_copy(g):
        lanes = slice(g * HPG * HD, (g + 1) * HPG * HD)
        return pltpu.make_async_copy(gq.at[:, lanes], gq_out.at[:, lanes], out_sem.at[g])

    for g in range(KVH):
        grads = stack(grad, g)
        outs = stack(o2, g)
        prob = probs[g]
        dots = jnp.sum(grads.astype(F32) * outs.astype(F32), axis=-1, keepdims=True)
        grad_weights = dot(grads, v2[:, head(g)], (1, 1))
        grad_scores = (prob * (grad_weights - dots) * SCALE).astype(BF16)
        for which, value in enumerate(
            (dot(grad_scores, stack(q2, g), (0, 0)), dot(prob.astype(BF16), grads, (0, 0)))
        ):
            own[g, which] = value
            for b in range(n - 1):
                part[b, g, which] = value[b * rows : (b + 1) * rows].astype(BF16)
        for d in range(n - 1, 0, -1):

            @pl.when(me >= 1 if d == 1 else me == n - 1)
            def _():
                part_copy(g, d, me - d).start()

        grad_query = dot(grad_scores, k2[:, head(g)], (1, 0)).astype(BF16)
        for h in range(HPG):
            gq[:, head(g * HPG + h)] = grad_query[h * rows : (h + 1) * rows]
        gq_copy(g).start()
        if g == 1:
            kv_forward((2, 3), 0)

    for d in range(1, n):
        gain_copy(d).wait_recv()
    total = gpart[me]
    for d in range(1, n):
        total += gland[d - 1]
    gshare[replica] = total

    def replica_copy(d, source):
        return pltpu.make_async_remote_copy(
            src_ref=gshare.at[source], dst_ref=gshare.at[source],
            send_sem=rep_send.at[d - 1], recv_sem=rep_recv.at[d - 1],
            device_id={"dp": lax.rem(replica + d, replicas)}, device_id_type=MESH,
        )

    for d in range(1, replicas):
        replica_copy(d, replica).start()

    for copy in locals_[4:]:
        copy.wait()
    squares = jnp.zeros((rows, HD), F32)
    kv_wait((2, 3), 0)
    for g in range(KVH):
        part_relay(g)
        prob, more = forward(q1, k1, v1, o1, g)
        squares += more
    inverse = inverse_of(squares)
    for h in range(QH):
        gain = gain_ref[:, head(h)].astype(F32)
        o1[:, head(h)] = (gain * o1[:, head(h)].astype(F32) * inverse).astype(BF16)
    normed = pltpu.make_async_remote_copy(
        src_ref=o1, dst_ref=next_out, send_sem=pipe_send.at[1], recv_sem=pipe_recv.at[1],
        device_id={"pipe": ahead}, device_id_type=MESH,
    )
    normed.start()

    for g in range(KVH):
        for d in range(1, min(2, n - 1) + 1):

            @pl.when(me + d < n)
            def _():
                part_copy(g, d, me).wait_recv()
                for which in range(2):
                    own[g, which, block(me), :] += land[d - 1, g, which].astype(F32)

        gk_out[:, head(g)] = own[g, 0, block(me), :].astype(BF16)
        gv_out[:, head(g)] = own[g, 1, block(me), :].astype(BF16)

    for d in range(1, replicas):
        replica_copy(d, lax.rem(replica + replicas - d, replicas)).wait_recv()
    total = gshare[0]
    for r in range(1, replicas):
        total += gshare[r]
    for h in range(share):
        gain_out[:, head(h)] = total[h : h + 1]

    for d in range(1, n):
        sent = me + d < n if d <= 2 else jnp.logical_and(me + 1 >= d, me + 1 < n)

        @pl.when(sent)
        def _():
            for g in range(KVH):
                for array in (0, 1):
                    kv_copy(array, g, d, me if d <= 2 else me + 1 - d).wait_send()
            for array in (2, 3):
                kv_copy(array, 0, d, me if d <= 2 else me + 1 - d).wait_send()

        @pl.when(me >= d)
        def _():
            for g in range(KVH):
                part_copy(g, d, me - d).wait_send()

        gain_copy(d).wait_send()
    for d in range(1, replicas):
        replica_copy(d, replica).wait_send()
    upstream.wait_send()
    for g in range(KVH):
        gq_copy(g).wait()
    normed.wait()


def write_out(*refs):
    count = len(refs) // 3
    sources, targets, held = refs[:count], refs[count : 2 * count], refs[2 * count : 3 * count]
    in_sem, out_sem = refs[3 * count :]
    reads = [pltpu.make_async_copy(sources[i], held[i], in_sem.at[i]) for i in range(count)]
    writes = [pltpu.make_async_copy(held[i], targets[i], out_sem.at[i]) for i in range(count)]
    for read in reads:
        read.start()
    for read, write in zip(reads, writes):
        read.wait()
        write.start()
    for write in writes:
        write.wait()


def local(n, pipes, replicas, q1, k1, v1, q2, k2, v2, go, gain):
    rows = q1.shape[2]
    length = n * rows
    share = QH // n
    args = [x[0, 0] for x in (q1, k1, v1, q2, k2, v2, go)] + [gain]
    anywhere = pl.BlockSpec(memory_space=pl.ANY)
    hbm = pl.BlockSpec(memory_space=pltpu.HBM)
    vmem = pl.BlockSpec(memory_space=pltpu.VMEM)
    wide = pltpu.VMEM((rows, WIDTH), BF16)
    keys = pltpu.VMEM((length, KVH * HD), BF16)
    dma = pltpu.SemaphoreType.DMA
    flops = 2 * 7 * rows * length * HD * QH
    outs = pl.pallas_call(
        functools.partial(kernel, n, pipes, replicas, rows),
        out_shape=(
            jax.ShapeDtypeStruct((rows, WIDTH), BF16),
            jax.ShapeDtypeStruct((rows, WIDTH), BF16),
            jax.ShapeDtypeStruct((rows, KVH * HD), BF16),
            jax.ShapeDtypeStruct((rows, KVH * HD), BF16),
            jax.ShapeDtypeStruct((1, WIDTH // n), F32),
        ),
        in_specs=[hbm] * 8,
        out_specs=(anywhere, anywhere, vmem, vmem, vmem),
        scratch_shapes=[
            pltpu.VMEM((1, WIDTH), BF16),
            wide, wide, wide, keys, keys, keys, keys,
            pltpu.VMEM((KVH, HPG * rows, length), F32),
            wide, wide, wide, wide,
            pltpu.VMEM((n, KVH, 2, rows, HD), BF16),
            pltpu.VMEM((KVH, 2, length, HD), F32),
            pltpu.VMEM((n - 1, KVH, 2, rows, HD), BF16),
            pltpu.VMEM((n, share, HD), F32),
            pltpu.VMEM((n - 1, share, HD), F32),
            pltpu.VMEM((replicas, share, HD), F32),
            dma((7,)),
            dma((4, KVH, n - 1)), dma((4, KVH, n - 1)),
            dma((KVH, n - 1)), dma((KVH, n - 1)),
            dma((KVH,)),
            dma((2,)), dma((2,)),
            dma((n - 1,)), dma((n - 1,)),
            dma((replicas - 1,)), dma((replicas - 1,)),
        ],
        compiler_params=pltpu.CompilerParams(
            collective_id=0, has_side_effects=True, vmem_limit_bytes=VMEM_LIMIT
        ),
        cost_estimate=pl.CostEstimate(flops=flops, bytes_accessed=8 * rows * WIDTH, transcendentals=0),
    )(*args)
    nxt, gq, gk, gv, gg = pl.pallas_call(
        write_out,
        out_shape=tuple(jax.ShapeDtypeStruct(x.shape, x.dtype) for x in outs),
        in_specs=[anywhere] * 5,
        out_specs=(hbm,) * 5,
        scratch_shapes=[pltpu.VMEM(x.shape, x.dtype) for x in outs] + [dma((5,)), dma((5,))],
        compiler_params=pltpu.CompilerParams(vmem_limit_bytes=VMEM_LIMIT),
    )(*outs)
    return nxt[None, None], gq[None, None], gk[None, None], gv[None, None], gg


def solution(mesh):
    tokens = P("dp", "pipe", "seq", None)
    sizes = (mesh.shape["seq"], mesh.shape["pipe"], mesh.shape["dp"])
    return jax.shard_map(
        functools.partial(local, *sizes),
        mesh=mesh,
        in_specs=(tokens,) * 7 + (P("pipe", None),),
        out_specs=(tokens,) * 4 + (P("pipe", "seq"),),
        check_vma=False,
    )
```

```python
import functools
import math

import jax
import jax.numpy as jnp
from jax import lax
from jax.experimental import pallas as pl
from jax.experimental.pallas import tpu as pltpu
from jax.sharding import PartitionSpec as P

QH = 32
KVH = 4
HD = 128
HPG = QH // KVH
WIDTH = QH * HD
EPS = 1e-05
SCALE = 1.0 / math.sqrt(HD)
SCALE_LOG2 = SCALE * math.log2(math.e)
VMEM_LIMIT = 60 * 1024 * 1024
HALF = KVH * HD // 2
MESH = pl.DeviceIdType.MESH
F32 = jnp.float32
BF16 = jnp.bfloat16


def head(h):
    return slice(h * HD, (h + 1) * HD)


def dot(a, b, contract):
    return lax.dot_general(a, b, ((contract[:1], contract[1:]), ((), ())), preferred_element_type=F32)


def kernel(
    n, pipes, replicas, rows,
    q1_in, k1_in, v1_in, q2_in, k2_in, v2_in, go_in, gain_in,
    next_out, gq_out, gk_out, gv_out, gain_out,
    gain_ref, q1, q2, up, k1, v1, k2, v2, probs, scores_grad, o1, o2, grad, gq, part, own, land,
    gpart, gland, gshare,
    local_sem, kv_send, kv_recv, part_send, part_recv, out_sem,
    pipe_send, pipe_recv, gain_send, gain_recv, rep_send, rep_recv,
):
    me = lax.axis_index("seq")
    section = lax.axis_index("pipe")
    replica = lax.axis_index("dp")
    length = n * rows
    behind = lax.rem(section + pipes - 1, pipes)
    ahead = lax.rem(section + 1, pipes)

    def block(b):
        return pl.ds(pl.multiple_of(b * rows, rows), rows)

    locals_ = [
        pltpu.make_async_copy(src, dst, local_sem.at[i])
        for i, (src, dst) in enumerate(
            (
                (q2_in, q2),
                (k2_in, k2.at[block(me)]),
                (v2_in, v2.at[block(me)]),
                (gain_in, gain_ref),
                (q1_in, q1),
                (k1_in, k1.at[block(me)]),
                (v1_in, v1.at[block(me)]),
            )
        )
    ]
    for copy in locals_:
        copy.start()

    barrier = pltpu.get_barrier_semaphore()
    for d in range(1, n):
        pl.semaphore_signal(barrier, inc=1, device_id={"seq": lax.rem(me + d, n)}, device_id_type=MESH)
    for d in range(1, replicas):
        pl.semaphore_signal(
            barrier, inc=1, device_id={"dp": lax.rem(replica + d, replicas)}, device_id_type=MESH
        )
    for other in (behind, ahead):
        pl.semaphore_signal(barrier, inc=1, device_id={"pipe": other}, device_id_type=MESH)

    for b in range(1, n):

        @pl.when(b > me)
        def _():
            for ref in (k1, v1, k2, v2):
                ref[b * rows : (b + 1) * rows, :] = jnp.zeros((rows, KVH * HD), BF16)

    pl.semaphore_wait(barrier, n - 1 + replicas - 1 + 2)

    def kv_copy(array, g, d, source):
        own_block = (k2_in, v2_in, k1_in, v1_in)[array]
        dst = (k2, v2, k1, v1)[array]
        lanes = head(g) if array < 2 else slice(g * HALF, (g + 1) * HALF)
        src = own_block.at[:, lanes] if d <= 2 else dst.at[block(source), lanes]
        return pltpu.make_async_remote_copy(
            src_ref=src,
            dst_ref=dst.at[block(source), lanes],
            send_sem=kv_send.at[array, g, d - 1],
            recv_sem=kv_recv.at[array, g, d - 1],
            device_id={"seq": lax.rem(me + (d if d <= 2 else 1), n)},
            device_id_type=MESH,
        )

    def kv_start(arrays, g, low, high):
        for d in range(min(2, n - 1), 0, -1):

            @pl.when(jnp.logical_and(me >= low, me < jnp.minimum(high, n - d)))
            def _():
                for array in arrays:
                    kv_copy(array, g, d, me).start()

    def kv_forward(arrays, g):
        for d in range(2, n - 1):

            @pl.when(jnp.logical_and(me >= d, me + 1 < n))
            def _():
                for array in arrays:
                    kv_copy(array, g, d, me - d).wait_recv()
                    kv_copy(array, g, d + 1, me - d).start()

    def kv_wait(arrays, g):
        for d in range(1, n):
            waits = me >= d if d == 1 else me == n - 1

            @pl.when(waits)
            def _():
                for array in arrays:
                    kv_copy(array, g, d, me - d).wait_recv()

    for g in range(KVH):
        kv_start((0, 1), g, 0, n)
    upstream = pltpu.make_async_remote_copy(
        src_ref=go_in, dst_ref=up, send_sem=pipe_send.at[0], recv_sem=pipe_recv.at[0],
        device_id={"pipe": behind}, device_id_type=MESH,
    )
    upstream.start()

    token = me * rows + lax.broadcasted_iota(jnp.int32, (rows, length), 0)
    allowed = (lax.broadcasted_iota(jnp.int32, (rows, length), 1) <= token)[None]

    def stack(ref, g):
        return jnp.concatenate([ref[:, head(g * HPG + h)] for h in range(HPG)], axis=0)

    def forward(q, k, v, o, g):
        scores = dot(stack(q, g), k[:, head(g)], (1, 1)).reshape(HPG, rows, length)
        scores = jnp.where(allowed, scores, -jnp.inf)
        highest = jnp.max(scores, axis=-1, keepdims=True)
        exponent = jnp.exp2((scores - highest) * SCALE_LOG2)
        prob = exponent * (1.0 / jnp.sum(exponent, axis=-1, keepdims=True))
        prob = prob.reshape(HPG * rows, length)
        out = dot(prob.astype(BF16), v[:, head(g)], (1, 0)).astype(BF16)
        squares = jnp.zeros((rows, HD), F32)
        for h in range(HPG):
            piece = out[h * rows : (h + 1) * rows]
            o[:, head(g * HPG + h)] = piece
            squares += piece.astype(F32) * piece.astype(F32)
        return prob, squares

    def inverse_of(squares):
        return lax.rsqrt(jnp.sum(squares, axis=-1, keepdims=True) * (1.0 / WIDTH) + EPS)

    for copy in locals_[:4]:
        copy.wait()
    squares = jnp.zeros((rows, HD), F32)
    kv_forward((0, 1), 0)
    for g in range(KVH):
        if g + 1 < KVH:
            kv_forward((0, 1), g + 1)
        kv_wait((0, 1), g)
        prob, more = forward(q2, k2, v2, o2, g)
        probs[g] = prob
        squares += more
    inverse = inverse_of(squares)

    upstream.wait_recv()
    cross = jnp.zeros((rows, HD), F32)
    share = QH // n
    for h in range(QH):
        activity = o2[:, head(h)].astype(F32)
        product = up[:, head(h)].astype(F32) * activity
        cross += gain_ref[:, head(h)].astype(F32) * product
        gpart[h // share, h % share : h % share + 1, :] = jnp.sum(product * inverse, axis=0, keepdims=True)
    cross_mean = jnp.sum(cross, axis=-1, keepdims=True) * (1.0 / WIDTH)
    factor = inverse * inverse * inverse * cross_mean
    for h in range(QH):
        gained = gain_ref[:, head(h)].astype(F32) * up[:, head(h)].astype(F32)
        grad[:, head(h)] = (gained * inverse - o2[:, head(h)].astype(F32) * factor).astype(BF16)

    def gain_copy(d):
        owner = lax.rem(me + d, n)
        return pltpu.make_async_remote_copy(
            src_ref=gpart.at[owner], dst_ref=gland.at[d - 1],
            send_sem=gain_send.at[d - 1], recv_sem=gain_recv.at[d - 1],
            device_id={"seq": owner}, device_id_type=MESH,
        )

    for half in range(2):
        kv_start((2, 3), half, 1, n)
    for d in range(1, n):
        gain_copy(d).start()

    def part_copy(g, d, target):
        return pltpu.make_async_remote_copy(
            src_ref=part.at[target, g], dst_ref=land.at[d - 1, g],
            send_sem=part_send.at[g, d - 1], recv_sem=part_recv.at[g, d - 1],
            device_id={"seq": lax.rem(me + n - (d if d <= 2 else 1), n)}, device_id_type=MESH,
        )

    def part_relay(g):
        for d in range(n - 2, 1, -1):

            @pl.when(jnp.logical_and(me >= d, me + 1 < n))
            def _():
                target = me - d
                part_copy(g, d + 1, target).wait_recv()
                for which in range(2):
                    total = own[g, which, block(target), :] + land[d, g, which].astype(F32)
                    part[target, g, which] = total.astype(BF16)
                part_copy(g, d, target).start()

    def gq_copy(g):
        lanes = slice(g * HPG * HD, (g + 1) * HPG * HD)
        return pltpu.make_async_copy(gq.at[:, lanes], gq_out.at[:, lanes], out_sem.at[g])

    for g in range(KVH):
        grads = stack(grad, g)
        outs = stack(o2, g)
        prob = probs[g]
        dots = jnp.sum(grads.astype(F32) * outs.astype(F32), axis=-1, keepdims=True)
        grad_weights = dot(grads, v2[:, head(g)], (1, 1))
        grad_scores = (prob * (grad_weights - dots) * SCALE).astype(BF16)
        scores_grad[g] = grad_scores
        for which, value in enumerate(
            (dot(grad_scores, stack(q2, g), (0, 0)), dot(prob.astype(BF16), grads, (0, 0)))
        ):
            own[g, which] = value
            for b in range(n - 1):
                part[b, g, which] = value[b * rows : (b + 1) * rows].astype(BF16)
        for d in range(n - 1, 0, -1):

            @pl.when(me >= 1 if d == 1 else me == n - 1)
            def _():
                part_copy(g, d, me - d).start()

        if g == 1:
            for half in range(2):
                kv_start((2, 3), half, 0, 1)
        if g >= 2:
            kv_forward((2, 3), g - 2)

    for g in range(KVH):
        grad_query = dot(scores_grad[g], k2[:, head(g)], (1, 0)).astype(BF16)
        for h in range(HPG):
            gq[:, head(g * HPG + h)] = grad_query[h * rows : (h + 1) * rows]
        gq_copy(g).start()

    for d in range(1, n):
        gain_copy(d).wait_recv()
    total = gpart[me]
    for d in range(1, n):
        total += gland[d - 1]
    gshare[replica] = total

    def replica_copy(d, source):
        return pltpu.make_async_remote_copy(
            src_ref=gshare.at[source], dst_ref=gshare.at[source],
            send_sem=rep_send.at[d - 1], recv_sem=rep_recv.at[d - 1],
            device_id={"dp": lax.rem(replica + d, replicas)}, device_id_type=MESH,
        )

    for d in range(1, replicas):
        replica_copy(d, replica).start()

    for copy in locals_[4:]:
        copy.wait()
    squares = jnp.zeros((rows, HD), F32)
    for g in range(KVH):
        part_relay(g)
    for g in range(KVH):
        if g % 2 == 0:
            kv_wait((2, 3), g // 2)
        prob, more = forward(q1, k1, v1, o1, g)
        squares += more
    inverse = inverse_of(squares)
    def normed_copy(g):
        lanes = slice(g * HPG * HD, (g + 1) * HPG * HD)
        return pltpu.make_async_remote_copy(
            src_ref=o1.at[:, lanes], dst_ref=next_out.at[:, lanes],
            send_sem=pipe_send.at[1 + g], recv_sem=pipe_recv.at[1 + g],
            device_id={"pipe": ahead}, device_id_type=MESH,
        )

    for g in range(KVH):
        for h in range(g * HPG, (g + 1) * HPG):
            gain = gain_ref[:, head(h)].astype(F32)
            o1[:, head(h)] = (gain * o1[:, head(h)].astype(F32) * inverse).astype(BF16)
        normed_copy(g).start()

    for g in range(KVH):
        for d in range(1, min(2, n - 1) + 1):

            @pl.when(me + d < n)
            def _():
                part_copy(g, d, me).wait_recv()
                for which in range(2):
                    own[g, which, block(me), :] += land[d - 1, g, which].astype(F32)

        gk_out[:, head(g)] = own[g, 0, block(me), :].astype(BF16)
        gv_out[:, head(g)] = own[g, 1, block(me), :].astype(BF16)

    for d in range(1, replicas):
        replica_copy(d, lax.rem(replica + replicas - d, replicas)).wait_recv()
    total = gshare[0]
    for r in range(1, replicas):
        total += gshare[r]
    for h in range(share):
        gain_out[:, head(h)] = total[h : h + 1]

    for d in range(1, n):
        sent = me + d < n if d <= 2 else jnp.logical_and(me + 1 >= d, me + 1 < n)

        @pl.when(sent)
        def _():
            for g in range(KVH):
                for array in (0, 1):
                    kv_copy(array, g, d, me if d <= 2 else me + 1 - d).wait_send()
            for half in range(2):
                for array in (2, 3):
                    kv_copy(array, half, d, me if d <= 2 else me + 1 - d).wait_send()

        @pl.when(me >= d)
        def _():
            for g in range(KVH):
                part_copy(g, d, me - d).wait_send()

        gain_copy(d).wait_send()
    for d in range(1, replicas):
        replica_copy(d, replica).wait_send()
    upstream.wait_send()
    for g in range(KVH):
        gq_copy(g).wait()
        normed_copy(g).wait()


def write_out(*refs):
    count = len(refs) // 3
    sources, targets, held = refs[:count], refs[count : 2 * count], refs[2 * count : 3 * count]
    in_sem, out_sem = refs[3 * count :]
    reads = [pltpu.make_async_copy(sources[i], held[i], in_sem.at[i]) for i in range(count)]
    writes = [pltpu.make_async_copy(held[i], targets[i], out_sem.at[i]) for i in range(count)]
    for read in reads:
        read.start()
    for read, write in zip(reads, writes):
        read.wait()
        write.start()
    for write in writes:
        write.wait()


def local(n, pipes, replicas, q1, k1, v1, q2, k2, v2, go, gain):
    rows = q1.shape[2]
    length = n * rows
    share = QH // n
    args = [x[0, 0] for x in (q1, k1, v1, q2, k2, v2, go)] + [gain]
    anywhere = pl.BlockSpec(memory_space=pl.ANY)
    hbm = pl.BlockSpec(memory_space=pltpu.HBM)
    vmem = pl.BlockSpec(memory_space=pltpu.VMEM)
    wide = pltpu.VMEM((rows, WIDTH), BF16)
    keys = pltpu.VMEM((length, KVH * HD), BF16)
    dma = pltpu.SemaphoreType.DMA
    flops = 2 * 7 * rows * length * HD * QH
    outs = pl.pallas_call(
        functools.partial(kernel, n, pipes, replicas, rows),
        out_shape=(
            jax.ShapeDtypeStruct((rows, WIDTH), BF16),
            jax.ShapeDtypeStruct((rows, WIDTH), BF16),
            jax.ShapeDtypeStruct((rows, KVH * HD), BF16),
            jax.ShapeDtypeStruct((rows, KVH * HD), BF16),
            jax.ShapeDtypeStruct((1, WIDTH // n), F32),
        ),
        in_specs=[hbm] * 8,
        out_specs=(anywhere, anywhere, vmem, vmem, vmem),
        scratch_shapes=[
            pltpu.VMEM((1, WIDTH), BF16),
            wide, wide, wide, keys, keys, keys, keys,
            pltpu.VMEM((KVH, HPG * rows, length), F32),
            pltpu.VMEM((KVH, HPG * rows, length), BF16),
            wide, wide, wide, wide,
            pltpu.VMEM((n, KVH, 2, rows, HD), BF16),
            pltpu.VMEM((KVH, 2, length, HD), F32),
            pltpu.VMEM((n - 1, KVH, 2, rows, HD), BF16),
            pltpu.VMEM((n, share, HD), F32),
            pltpu.VMEM((n - 1, share, HD), F32),
            pltpu.VMEM((replicas, share, HD), F32),
            dma((7,)),
            dma((4, KVH, n - 1)), dma((4, KVH, n - 1)),
            dma((KVH, n - 1)), dma((KVH, n - 1)),
            dma((KVH,)),
            dma((1 + KVH,)), dma((1 + KVH,)),
            dma((n - 1,)), dma((n - 1,)),
            dma((replicas - 1,)), dma((replicas - 1,)),
        ],
        compiler_params=pltpu.CompilerParams(
            collective_id=0, has_side_effects=True, vmem_limit_bytes=VMEM_LIMIT
        ),
        cost_estimate=pl.CostEstimate(flops=flops, bytes_accessed=8 * rows * WIDTH, transcendentals=0),
    )(*args)
    nxt, gq, gk, gv, gg = pl.pallas_call(
        write_out,
        out_shape=tuple(jax.ShapeDtypeStruct(x.shape, x.dtype) for x in outs),
        in_specs=[anywhere] * 5,
        out_specs=(hbm,) * 5,
        scratch_shapes=[pltpu.VMEM(x.shape, x.dtype) for x in outs] + [dma((5,)), dma((5,))],
        compiler_params=pltpu.CompilerParams(vmem_limit_bytes=VMEM_LIMIT),
    )(*outs)
    return nxt[None, None], gq[None, None], gk[None, None], gv[None, None], gg


def solution(mesh):
    tokens = P("dp", "pipe", "seq", None)
    sizes = (mesh.shape["seq"], mesh.shape["pipe"], mesh.shape["dp"])
    return jax.shard_map(
        functools.partial(local, *sizes),
        mesh=mesh,
        in_specs=(tokens,) * 7 + (P("pipe", None),),
        out_specs=(tokens,) * 4 + (P("pipe", "seq"),),
        check_vma=False,
    )
```

```python
import functools
import math

import jax
import jax.numpy as jnp
from jax import lax
from jax.experimental import pallas as pl
from jax.experimental.pallas import tpu as pltpu
from jax.sharding import PartitionSpec as P

QH = 32
KVH = 4
HD = 128
HPG = QH // KVH
WIDTH = QH * HD
EPS = 1e-05
SCALE = 1.0 / math.sqrt(HD)
SCALE_LOG2 = SCALE * math.log2(math.e)
VMEM_LIMIT = 60 * 1024 * 1024
HALF = KVH * HD // 2
MESH = pl.DeviceIdType.MESH
F32 = jnp.float32
BF16 = jnp.bfloat16


def head(h):
    return slice(h * HD, (h + 1) * HD)


def dot(a, b, contract):
    return lax.dot_general(a, b, ((contract[:1], contract[1:]), ((), ())), preferred_element_type=F32)


def kernel(
    n, pipes, replicas, rows,
    q1_in, k1_in, v1_in, q2_in, k2_in, v2_in, go_in, gain_in,
    next_out, gq_out, gk_out, gv_out, gain_out,
    gain_ref, q1, q2, up, k1, v1, k2, v2, bias, probs, scores_grad, o1, o2, grad, gq, part, own, land,
    gpart, gland, gshare,
    local_sem, kv_send, kv_recv, part_send, part_recv, out_sem,
    pipe_send, pipe_recv, gain_send, gain_recv, rep_send, rep_recv,
):
    me = lax.axis_index("seq")
    section = lax.axis_index("pipe")
    replica = lax.axis_index("dp")
    length = n * rows
    behind = lax.rem(section + pipes - 1, pipes)
    ahead = lax.rem(section + 1, pipes)

    def block(b):
        return pl.ds(pl.multiple_of(b * rows, rows), rows)

    locals_ = [
        pltpu.make_async_copy(src, dst, local_sem.at[i])
        for i, (src, dst) in enumerate(
            (
                (q2_in, q2),
                (k2_in, k2.at[block(me)]),
                (v2_in, v2.at[block(me)]),
                (gain_in, gain_ref),
                (q1_in, q1),
                (k1_in, k1.at[block(me)]),
                (v1_in, v1.at[block(me)]),
            )
        )
    ]
    for copy in locals_:
        copy.start()

    barrier = pltpu.get_barrier_semaphore()
    for d in range(1, n):
        pl.semaphore_signal(barrier, inc=1, device_id={"seq": lax.rem(me + d, n)}, device_id_type=MESH)
    for d in range(1, replicas):
        pl.semaphore_signal(
            barrier, inc=1, device_id={"dp": lax.rem(replica + d, replicas)}, device_id_type=MESH
        )
    for other in (behind, ahead):
        pl.semaphore_signal(barrier, inc=1, device_id={"pipe": other}, device_id_type=MESH)

    for b in range(1, n):

        @pl.when(b > me)
        def _():
            for ref in (k1, v1, k2, v2):
                ref[b * rows : (b + 1) * rows, :] = jnp.zeros((rows, KVH * HD), BF16)

    pl.semaphore_wait(barrier, n - 1 + replicas - 1 + 2)

    def kv_copy(array, g, d, source):
        own_block = (k2_in, v2_in, k1_in, v1_in)[array]
        dst = (k2, v2, k1, v1)[array]
        lanes = head(g) if array < 2 else slice(g * HALF, (g + 1) * HALF)
        src = own_block.at[:, lanes] if d <= 2 else dst.at[block(source), lanes]
        return pltpu.make_async_remote_copy(
            src_ref=src,
            dst_ref=dst.at[block(source), lanes],
            send_sem=kv_send.at[array, g, d - 1],
            recv_sem=kv_recv.at[array, g, d - 1],
            device_id={"seq": lax.rem(me + (d if d <= 2 else 1), n)},
            device_id_type=MESH,
        )

    def kv_start(arrays, g, low, high):
        for d in range(min(2, n - 1), 0, -1):

            @pl.when(jnp.logical_and(me >= low, me < jnp.minimum(high, n - d)))
            def _():
                for array in arrays:
                    kv_copy(array, g, d, me).start()

    def kv_forward(arrays, g):
        for d in range(2, n - 1):

            @pl.when(jnp.logical_and(me >= d, me + 1 < n))
            def _():
                for array in arrays:
                    kv_copy(array, g, d, me - d).wait_recv()
                    kv_copy(array, g, d + 1, me - d).start()

    def kv_wait(arrays, g):
        for d in range(1, n):
            waits = me >= d if d == 1 else me == n - 1

            @pl.when(waits)
            def _():
                for array in arrays:
                    kv_copy(array, g, d, me - d).wait_recv()

    for g in range(KVH):
        kv_start((0, 1), g, 0, n)
    upstream = pltpu.make_async_remote_copy(
        src_ref=go_in, dst_ref=up, send_sem=pipe_send.at[0], recv_sem=pipe_recv.at[0],
        device_id={"pipe": behind}, device_id_type=MESH,
    )
    upstream.start()

    token = me * rows + lax.broadcasted_iota(jnp.int32, (rows, length), 0)
    bias[...] = jnp.where(lax.broadcasted_iota(jnp.int32, (rows, length), 1) <= token, 0.0, -jnp.inf)

    def stack(ref, g):
        return jnp.concatenate([ref[:, head(g * HPG + h)] for h in range(HPG)], axis=0)

    def forward(q, k, v, o, g, keep):
        scores = dot(stack(q, g), k[:, head(g)], (1, 1))
        weights = []
        for h in range(HPG):
            part_rows = slice(h * rows, (h + 1) * rows)
            score = scores[part_rows] + bias[...]
            highest = jnp.max(score, axis=-1, keepdims=True)
            exponent = jnp.exp2((score - highest) * SCALE_LOG2)
            prob = exponent * (1.0 / jnp.sum(exponent, axis=-1, keepdims=True))
            if keep:
                probs[g, part_rows, :] = prob
            weights.append(prob.astype(BF16))
        out = dot(jnp.concatenate(weights, axis=0), v[:, head(g)], (1, 0)).astype(BF16)
        squares = jnp.zeros((rows, HD), F32)
        for h in range(HPG):
            piece = out[h * rows : (h + 1) * rows]
            o[:, head(g * HPG + h)] = piece
            squares += piece.astype(F32) * piece.astype(F32)
        return squares

    def inverse_of(squares):
        return lax.rsqrt(jnp.sum(squares, axis=-1, keepdims=True) * (1.0 / WIDTH) + EPS)

    for copy in locals_[:4]:
        copy.wait()
    squares = jnp.zeros((rows, HD), F32)
    kv_forward((0, 1), 0)
    for g in range(KVH):
        if g + 1 < KVH:
            kv_forward((0, 1), g + 1)
        kv_wait((0, 1), g)
        squares += forward(q2, k2, v2, o2, g, True)
    inverse = inverse_of(squares)

    upstream.wait_recv()
    cross = jnp.zeros((rows, HD), F32)
    share = QH // n
    for h in range(QH):
        activity = o2[:, head(h)].astype(F32)
        product = up[:, head(h)].astype(F32) * activity
        cross += gain_ref[:, head(h)].astype(F32) * product
        gpart[h // share, h % share : h % share + 1, :] = jnp.sum(product * inverse, axis=0, keepdims=True)
    cross_mean = jnp.sum(cross, axis=-1, keepdims=True) * (1.0 / WIDTH)
    factor = inverse * inverse * inverse * cross_mean
    for h in range(QH):
        gained = gain_ref[:, head(h)].astype(F32) * up[:, head(h)].astype(F32)
        grad[:, head(h)] = (gained * inverse - o2[:, head(h)].astype(F32) * factor).astype(BF16)

    def gain_copy(d):
        owner = lax.rem(me + d, n)
        return pltpu.make_async_remote_copy(
            src_ref=gpart.at[owner], dst_ref=gland.at[d - 1],
            send_sem=gain_send.at[d - 1], recv_sem=gain_recv.at[d - 1],
            device_id={"seq": owner}, device_id_type=MESH,
        )

    for half in range(2):
        kv_start((2, 3), half, 1, n)
    for d in range(1, n):
        gain_copy(d).start()

    def part_copy(g, d, target):
        return pltpu.make_async_remote_copy(
            src_ref=part.at[target, g], dst_ref=land.at[d - 1, g],
            send_sem=part_send.at[g, d - 1], recv_sem=part_recv.at[g, d - 1],
            device_id={"seq": lax.rem(me + n - (d if d <= 2 else 1), n)}, device_id_type=MESH,
        )

    def part_relay(g):
        for d in range(n - 2, 1, -1):

            @pl.when(jnp.logical_and(me >= d, me + 1 < n))
            def _():
                target = me - d
                part_copy(g, d + 1, target).wait_recv()
                for which in range(2):
                    total = own[g, which, block(target), :] + land[d, g, which].astype(F32)
                    part[target, g, which] = total.astype(BF16)
                part_copy(g, d, target).start()

    def gq_copy(g):
        lanes = slice(g * HPG * HD, (g + 1) * HPG * HD)
        return pltpu.make_async_copy(gq.at[:, lanes], gq_out.at[:, lanes], out_sem.at[g])

    for g in range(KVH):
        grads = stack(grad, g)
        grad_weights = dot(grads, v2[:, head(g)], (1, 1))
        weights, grad_scores = [], []
        for h in range(HPG):
            part_rows = slice(h * rows, (h + 1) * rows)
            product = grad[:, head(g * HPG + h)].astype(F32) * o2[:, head(g * HPG + h)].astype(F32)
            dots = jnp.sum(product, axis=-1, keepdims=True)
            prob = probs[g, part_rows, :]
            score = (prob * (grad_weights[part_rows] - dots) * SCALE).astype(BF16)
            scores_grad[g, part_rows, :] = score
            grad_scores.append(score)
            weights.append(prob.astype(BF16))
        grad_scores = jnp.concatenate(grad_scores, axis=0)
        weights = jnp.concatenate(weights, axis=0)
        for which, value in enumerate(
            (dot(grad_scores, stack(q2, g), (0, 0)), dot(weights, grads, (0, 0)))
        ):
            own[g, which] = value
            for b in range(n - 1):
                part[b, g, which] = value[b * rows : (b + 1) * rows].astype(BF16)
        for d in range(n - 1, 0, -1):

            @pl.when(me >= 1 if d == 1 else me == n - 1)
            def _():
                part_copy(g, d, me - d).start()

        if g == 1:
            for half in range(2):
                kv_start((2, 3), half, 0, 1)
        if g >= 2:
            kv_forward((2, 3), g - 2)

    for g in range(KVH):
        grad_query = dot(scores_grad[g], k2[:, head(g)], (1, 0)).astype(BF16)
        for h in range(HPG):
            gq[:, head(g * HPG + h)] = grad_query[h * rows : (h + 1) * rows]
        gq_copy(g).start()

    for d in range(1, n):
        gain_copy(d).wait_recv()
    total = gpart[me]
    for d in range(1, n):
        total += gland[d - 1]
    gshare[replica] = total

    def replica_copy(d, source):
        return pltpu.make_async_remote_copy(
            src_ref=gshare.at[source], dst_ref=gshare.at[source],
            send_sem=rep_send.at[d - 1], recv_sem=rep_recv.at[d - 1],
            device_id={"dp": lax.rem(replica + d, replicas)}, device_id_type=MESH,
        )

    for d in range(1, replicas):
        replica_copy(d, replica).start()

    for copy in locals_[4:]:
        copy.wait()
    squares = jnp.zeros((rows, HD), F32)
    for g in range(KVH):
        part_relay(g)
    for g in range(KVH):
        if g % 2 == 0:
            kv_wait((2, 3), g // 2)
        squares += forward(q1, k1, v1, o1, g, False)
    inverse = inverse_of(squares)
    def normed_copy(g):
        lanes = slice(g * HPG * HD, (g + 1) * HPG * HD)
        return pltpu.make_async_remote_copy(
            src_ref=o1.at[:, lanes], dst_ref=next_out.at[:, lanes],
            send_sem=pipe_send.at[1 + g], recv_sem=pipe_recv.at[1 + g],
            device_id={"pipe": ahead}, device_id_type=MESH,
        )

    for g in range(KVH):
        for h in range(g * HPG, (g + 1) * HPG):
            gain = gain_ref[:, head(h)].astype(F32)
            o1[:, head(h)] = (gain * o1[:, head(h)].astype(F32) * inverse).astype(BF16)
        normed_copy(g).start()

    for g in range(KVH):
        for d in range(1, min(2, n - 1) + 1):

            @pl.when(me + d < n)
            def _():
                part_copy(g, d, me).wait_recv()
                for which in range(2):
                    own[g, which, block(me), :] += land[d - 1, g, which].astype(F32)

        gk_out[:, head(g)] = own[g, 0, block(me), :].astype(BF16)
        gv_out[:, head(g)] = own[g, 1, block(me), :].astype(BF16)

    for d in range(1, replicas):
        replica_copy(d, lax.rem(replica + replicas - d, replicas)).wait_recv()
    total = gshare[0]
    for r in range(1, replicas):
        total += gshare[r]
    for h in range(share):
        gain_out[:, head(h)] = total[h : h + 1]

    for d in range(1, n):
        sent = me + d < n if d <= 2 else jnp.logical_and(me + 1 >= d, me + 1 < n)

        @pl.when(sent)
        def _():
            for g in range(KVH):
                for array in (0, 1):
                    kv_copy(array, g, d, me if d <= 2 else me + 1 - d).wait_send()
            for half in range(2):
                for array in (2, 3):
                    kv_copy(array, half, d, me if d <= 2 else me + 1 - d).wait_send()

        @pl.when(me >= d)
        def _():
            for g in range(KVH):
                part_copy(g, d, me - d).wait_send()

        gain_copy(d).wait_send()
    for d in range(1, replicas):
        replica_copy(d, replica).wait_send()
    upstream.wait_send()
    for g in range(KVH):
        gq_copy(g).wait()
        normed_copy(g).wait()


def write_out(*refs):
    count = len(refs) // 3
    sources, targets, held = refs[:count], refs[count : 2 * count], refs[2 * count : 3 * count]
    in_sem, out_sem = refs[3 * count :]
    reads = [pltpu.make_async_copy(sources[i], held[i], in_sem.at[i]) for i in range(count)]
    writes = [pltpu.make_async_copy(held[i], targets[i], out_sem.at[i]) for i in range(count)]
    for read in reads:
        read.start()
    for read, write in zip(reads, writes):
        read.wait()
        write.start()
    for write in writes:
        write.wait()


def local(n, pipes, replicas, q1, k1, v1, q2, k2, v2, go, gain):
    rows = q1.shape[2]
    length = n * rows
    share = QH // n
    args = [x[0, 0] for x in (q1, k1, v1, q2, k2, v2, go)] + [gain]
    anywhere = pl.BlockSpec(memory_space=pl.ANY)
    hbm = pl.BlockSpec(memory_space=pltpu.HBM)
    vmem = pl.BlockSpec(memory_space=pltpu.VMEM)
    wide = pltpu.VMEM((rows, WIDTH), BF16)
    keys = pltpu.VMEM((length, KVH * HD), BF16)
    dma = pltpu.SemaphoreType.DMA
    flops = 2 * 7 * rows * length * HD * QH
    outs = pl.pallas_call(
        functools.partial(kernel, n, pipes, replicas, rows),
        out_shape=(
            jax.ShapeDtypeStruct((rows, WIDTH), BF16),
            jax.ShapeDtypeStruct((rows, WIDTH), BF16),
            jax.ShapeDtypeStruct((rows, KVH * HD), BF16),
            jax.ShapeDtypeStruct((rows, KVH * HD), BF16),
            jax.ShapeDtypeStruct((1, WIDTH // n), F32),
        ),
        in_specs=[hbm] * 8,
        out_specs=(anywhere, anywhere, vmem, vmem, vmem),
        scratch_shapes=[
            pltpu.VMEM((1, WIDTH), BF16),
            wide, wide, wide, keys, keys, keys, keys,
            pltpu.VMEM((rows, length), F32),
            pltpu.VMEM((KVH, HPG * rows, length), F32),
            pltpu.VMEM((KVH, HPG * rows, length), BF16),
            wide, wide, wide, wide,
            pltpu.VMEM((n, KVH, 2, rows, HD), BF16),
            pltpu.VMEM((KVH, 2, length, HD), F32),
            pltpu.VMEM((n - 1, KVH, 2, rows, HD), BF16),
            pltpu.VMEM((n, share, HD), F32),
            pltpu.VMEM((n - 1, share, HD), F32),
            pltpu.VMEM((replicas, share, HD), F32),
            dma((7,)),
            dma((4, KVH, n - 1)), dma((4, KVH, n - 1)),
            dma((KVH, n - 1)), dma((KVH, n - 1)),
            dma((KVH,)),
            dma((1 + KVH,)), dma((1 + KVH,)),
            dma((n - 1,)), dma((n - 1,)),
            dma((replicas - 1,)), dma((replicas - 1,)),
        ],
        compiler_params=pltpu.CompilerParams(
            collective_id=0, has_side_effects=True, vmem_limit_bytes=VMEM_LIMIT
        ),
        cost_estimate=pl.CostEstimate(flops=flops, bytes_accessed=8 * rows * WIDTH, transcendentals=0),
    )(*args)
    nxt, gq, gk, gv, gg = pl.pallas_call(
        write_out,
        out_shape=tuple(jax.ShapeDtypeStruct(x.shape, x.dtype) for x in outs),
        in_specs=[anywhere] * 5,
        out_specs=(hbm,) * 5,
        scratch_shapes=[pltpu.VMEM(x.shape, x.dtype) for x in outs] + [dma((5,)), dma((5,))],
        compiler_params=pltpu.CompilerParams(vmem_limit_bytes=VMEM_LIMIT),
    )(*outs)
    return nxt[None, None], gq[None, None], gk[None, None], gv[None, None], gg


def solution(mesh):
    tokens = P("dp", "pipe", "seq", None)
    sizes = (mesh.shape["seq"], mesh.shape["pipe"], mesh.shape["dp"])
    return jax.shard_map(
        functools.partial(local, *sizes),
        mesh=mesh,
        in_specs=(tokens,) * 7 + (P("pipe", None),),
        out_specs=(tokens,) * 4 + (P("pipe", "seq"),),
        check_vma=False,
    )
```

```python
import functools
import math

import jax
import jax.numpy as jnp
from jax import lax
from jax.experimental import pallas as pl
from jax.experimental.pallas import tpu as pltpu
from jax.sharding import PartitionSpec as P

QH = 32
KVH = 4
HD = 128
HPG = QH // KVH
WIDTH = QH * HD
EPS = 1e-05
SCALE = 1.0 / math.sqrt(HD)
SCALE_LOG2 = SCALE * math.log2(math.e)
VMEM_LIMIT = 60 * 1024 * 1024
HALF = KVH * HD // 2
MESH = pl.DeviceIdType.MESH
F32 = jnp.float32
BF16 = jnp.bfloat16


def head(h):
    return slice(h * HD, (h + 1) * HD)


def dot(a, b, contract):
    return lax.dot_general(a, b, ((contract[:1], contract[1:]), ((), ())), preferred_element_type=F32)


def kernel(
    n, pipes, replicas, rows,
    q1_in, k1_in, v1_in, q2_in, k2_in, v2_in, go_in, gain_in,
    next_out, gq_out, gk_out, gv_out, gain_out,
    gain_ref, q1, q2, up, k1, v1, k2, v2, bias, probs, scores_grad, o1, o2, grad, gq, part, own, land,
    gpart, gland, gshare,
    local_sem, kv_send, kv_recv, part_send, part_recv, out_sem,
    pipe_send, pipe_recv, gain_send, gain_recv, rep_send, rep_recv,
):
    me = lax.axis_index("seq")
    section = lax.axis_index("pipe")
    replica = lax.axis_index("dp")
    length = n * rows
    behind = lax.rem(section + pipes - 1, pipes)
    ahead = lax.rem(section + 1, pipes)

    def block(b):
        return pl.ds(pl.multiple_of(b * rows, rows), rows)

    locals_ = [
        pltpu.make_async_copy(src, dst, local_sem.at[i])
        for i, (src, dst) in enumerate(
            (
                (q2_in, q2),
                (k2_in, k2.at[block(me)]),
                (v2_in, v2.at[block(me)]),
                (gain_in, gain_ref),
                (q1_in, q1),
                (k1_in, k1.at[block(me)]),
                (v1_in, v1.at[block(me)]),
            )
        )
    ]
    for copy in locals_:
        copy.start()

    barrier = pltpu.get_barrier_semaphore()
    for d in range(1, n):
        pl.semaphore_signal(barrier, inc=1, device_id={"seq": lax.rem(me + d, n)}, device_id_type=MESH)
    for d in range(1, replicas):
        pl.semaphore_signal(
            barrier, inc=1, device_id={"dp": lax.rem(replica + d, replicas)}, device_id_type=MESH
        )
    for other in (behind, ahead):
        pl.semaphore_signal(barrier, inc=1, device_id={"pipe": other}, device_id_type=MESH)

    for b in range(1, n):

        @pl.when(b > me)
        def _():
            for ref in (k1, v1, k2, v2):
                ref[b * rows : (b + 1) * rows, :] = jnp.zeros((rows, KVH * HD), BF16)

    for copy in locals_[:4]:
        copy.wait()
    pl.semaphore_wait(barrier, n - 1 + replicas - 1 + 2)

    def kv_copy(array, g, d, source):
        dst = (k2, v2, k1, v1)[array]
        lanes = head(g) if array < 2 else slice(g * HALF, (g + 1) * HALF)
        return pltpu.make_async_remote_copy(
            src_ref=dst.at[block(source), lanes],
            dst_ref=dst.at[block(source), lanes],
            send_sem=kv_send.at[array, g, d - 1],
            recv_sem=kv_recv.at[array, g, d - 1],
            device_id={"seq": lax.rem(me + (d if d <= 2 else 1), n)},
            device_id_type=MESH,
        )

    def kv_start(arrays, g, low, high):
        for d in range(min(2, n - 1), 0, -1):

            @pl.when(jnp.logical_and(me >= low, me < jnp.minimum(high, n - d)))
            def _():
                for array in arrays:
                    kv_copy(array, g, d, me).start()

    def kv_forward(arrays, g):
        for d in range(2, n - 1):

            @pl.when(jnp.logical_and(me >= d, me + 1 < n))
            def _():
                for array in arrays:
                    kv_copy(array, g, d, me - d).wait_recv()
                    kv_copy(array, g, d + 1, me - d).start()

    def kv_wait(arrays, g):
        for d in range(1, n):
            waits = me >= d if d == 1 else me == n - 1

            @pl.when(waits)
            def _():
                for array in arrays:
                    kv_copy(array, g, d, me - d).wait_recv()

    for g in range(KVH):
        kv_start((0, 1), g, 0, n)
    upstream = pltpu.make_async_remote_copy(
        src_ref=go_in, dst_ref=up, send_sem=pipe_send.at[0], recv_sem=pipe_recv.at[0],
        device_id={"pipe": behind}, device_id_type=MESH,
    )
    upstream.start()

    token = me * rows + lax.broadcasted_iota(jnp.int32, (rows, length), 0)
    bias[...] = jnp.where(lax.broadcasted_iota(jnp.int32, (rows, length), 1) <= token, 0.0, -jnp.inf)

    def stack(ref, g):
        return jnp.concatenate([ref[:, head(g * HPG + h)] for h in range(HPG)], axis=0)

    def forward(q, k, v, o, g, keep):
        scores = dot(stack(q, g), k[:, head(g)], (1, 1))
        weights = []
        for h in range(HPG):
            part_rows = slice(h * rows, (h + 1) * rows)
            score = scores[part_rows] + bias[...]
            highest = jnp.max(score, axis=-1, keepdims=True)
            exponent = jnp.exp2((score - highest) * SCALE_LOG2)
            prob = exponent * (1.0 / jnp.sum(exponent, axis=-1, keepdims=True))
            if keep:
                probs[g, part_rows, :] = prob
            weights.append(prob.astype(BF16))
        out = dot(jnp.concatenate(weights, axis=0), v[:, head(g)], (1, 0)).astype(BF16)
        squares = jnp.zeros((rows, HD), F32)
        for h in range(HPG):
            piece = out[h * rows : (h + 1) * rows]
            o[:, head(g * HPG + h)] = piece
            squares += piece.astype(F32) * piece.astype(F32)
        return squares

    def inverse_of(squares):
        return lax.rsqrt(jnp.sum(squares, axis=-1, keepdims=True) * (1.0 / WIDTH) + EPS)

    squares = jnp.zeros((rows, HD), F32)
    kv_forward((0, 1), 0)
    for g in range(KVH):
        if g + 1 < KVH:
            kv_forward((0, 1), g + 1)
        kv_wait((0, 1), g)
        squares += forward(q2, k2, v2, o2, g, True)
    inverse = inverse_of(squares)

    upstream.wait_recv()
    cross = jnp.zeros((rows, HD), F32)
    share = QH // n
    for h in range(QH):
        activity = o2[:, head(h)].astype(F32)
        product = up[:, head(h)].astype(F32) * activity
        cross += gain_ref[:, head(h)].astype(F32) * product
        gpart[h // share, h % share : h % share + 1, :] = jnp.sum(product * inverse, axis=0, keepdims=True)
    cross_mean = jnp.sum(cross, axis=-1, keepdims=True) * (1.0 / WIDTH)
    factor = inverse * inverse * inverse * cross_mean
    for h in range(QH):
        gained = gain_ref[:, head(h)].astype(F32) * up[:, head(h)].astype(F32)
        grad[:, head(h)] = (gained * inverse - o2[:, head(h)].astype(F32) * factor).astype(BF16)

    def gain_copy(d):
        owner = lax.rem(me + d, n)
        return pltpu.make_async_remote_copy(
            src_ref=gpart.at[owner], dst_ref=gland.at[d - 1],
            send_sem=gain_send.at[d - 1], recv_sem=gain_recv.at[d - 1],
            device_id={"seq": owner}, device_id_type=MESH,
        )

    for copy in locals_[4:]:
        copy.wait()
    for half in range(2):
        kv_start((2, 3), half, 1, n)
    for d in range(1, n):
        gain_copy(d).start()

    def part_copy(g, d, target):
        return pltpu.make_async_remote_copy(
            src_ref=part.at[target, g], dst_ref=land.at[d - 1, g],
            send_sem=part_send.at[g, d - 1], recv_sem=part_recv.at[g, d - 1],
            device_id={"seq": lax.rem(me + n - (d if d <= 2 else 1), n)}, device_id_type=MESH,
        )

    def part_relay(g):
        for d in range(n - 2, 1, -1):

            @pl.when(jnp.logical_and(me >= d, me + 1 < n))
            def _():
                target = me - d
                part_copy(g, d + 1, target).wait_recv()
                for which in range(2):
                    total = own[g, which, block(target), :] + land[d, g, which].astype(F32)
                    part[target, g, which] = total.astype(BF16)
                part_copy(g, d, target).start()

    def gq_copy(g):
        lanes = slice(g * HPG * HD, (g + 1) * HPG * HD)
        return pltpu.make_async_copy(gq.at[:, lanes], gq_out.at[:, lanes], out_sem.at[g])

    for g in range(KVH):
        grads = stack(grad, g)
        grad_weights = dot(grads, v2[:, head(g)], (1, 1))
        weights, grad_scores = [], []
        for h in range(HPG):
            part_rows = slice(h * rows, (h + 1) * rows)
            product = grad[:, head(g * HPG + h)].astype(F32) * o2[:, head(g * HPG + h)].astype(F32)
            dots = jnp.sum(product, axis=-1, keepdims=True)
            prob = probs[g, part_rows, :]
            score = (prob * (grad_weights[part_rows] - dots) * SCALE).astype(BF16)
            scores_grad[g, part_rows, :] = score
            grad_scores.append(score)
            weights.append(prob.astype(BF16))
        grad_scores = jnp.concatenate(grad_scores, axis=0)
        weights = jnp.concatenate(weights, axis=0)
        for which, value in enumerate(
            (dot(grad_scores, stack(q2, g), (0, 0)), dot(weights, grads, (0, 0)))
        ):
            own[g, which] = value
            for b in range(n - 1):
                part[b, g, which] = value[b * rows : (b + 1) * rows].astype(BF16)
        for d in range(n - 1, 0, -1):

            @pl.when(me >= 1 if d == 1 else me == n - 1)
            def _():
                part_copy(g, d, me - d).start()

        if g == 1:
            for half in range(2):
                kv_start((2, 3), half, 0, 1)
        if g >= 2:
            kv_forward((2, 3), g - 2)

    for g in range(KVH):
        grad_query = dot(scores_grad[g], k2[:, head(g)], (1, 0)).astype(BF16)
        for h in range(HPG):
            gq[:, head(g * HPG + h)] = grad_query[h * rows : (h + 1) * rows]
        gq_copy(g).start()
        part_relay(g)

    for d in range(1, n):
        gain_copy(d).wait_recv()
    total = gpart[me]
    for d in range(1, n):
        total += gland[d - 1]
    gshare[replica] = total

    def replica_copy(d, source):
        return pltpu.make_async_remote_copy(
            src_ref=gshare.at[source], dst_ref=gshare.at[source],
            send_sem=rep_send.at[d - 1], recv_sem=rep_recv.at[d - 1],
            device_id={"dp": lax.rem(replica + d, replicas)}, device_id_type=MESH,
        )

    for d in range(1, replicas):
        replica_copy(d, replica).start()

    squares = jnp.zeros((rows, HD), F32)
    for g in range(KVH):
        if g % 2 == 0:
            kv_wait((2, 3), g // 2)
        squares += forward(q1, k1, v1, o1, g, False)
    inverse = inverse_of(squares)
    def normed_copy(g):
        lanes = slice(g * HPG * HD, (g + 1) * HPG * HD)
        return pltpu.make_async_remote_copy(
            src_ref=o1.at[:, lanes], dst_ref=next_out.at[:, lanes],
            send_sem=pipe_send.at[1 + g], recv_sem=pipe_recv.at[1 + g],
            device_id={"pipe": ahead}, device_id_type=MESH,
        )

    for g in range(KVH):
        for h in range(g * HPG, (g + 1) * HPG):
            gain = gain_ref[:, head(h)].astype(F32)
            o1[:, head(h)] = (gain * o1[:, head(h)].astype(F32) * inverse).astype(BF16)
        normed_copy(g).start()

    for g in range(KVH):
        for d in range(1, min(2, n - 1) + 1):

            @pl.when(me + d < n)
            def _():
                part_copy(g, d, me).wait_recv()
                for which in range(2):
                    own[g, which, block(me), :] += land[d - 1, g, which].astype(F32)

        gk_out[:, head(g)] = own[g, 0, block(me), :].astype(BF16)
        gv_out[:, head(g)] = own[g, 1, block(me), :].astype(BF16)

    for d in range(1, replicas):
        replica_copy(d, lax.rem(replica + replicas - d, replicas)).wait_recv()
    total = gshare[0]
    for r in range(1, replicas):
        total += gshare[r]
    for h in range(share):
        gain_out[:, head(h)] = total[h : h + 1]

    for d in range(1, n):
        sent = me + d < n if d <= 2 else jnp.logical_and(me + 1 >= d, me + 1 < n)

        @pl.when(sent)
        def _():
            for g in range(KVH):
                for array in (0, 1):
                    kv_copy(array, g, d, me if d <= 2 else me + 1 - d).wait_send()
            for half in range(2):
                for array in (2, 3):
                    kv_copy(array, half, d, me if d <= 2 else me + 1 - d).wait_send()

        @pl.when(me >= d)
        def _():
            for g in range(KVH):
                part_copy(g, d, me - d).wait_send()

        gain_copy(d).wait_send()
    for d in range(1, replicas):
        replica_copy(d, replica).wait_send()
    upstream.wait_send()
    for g in range(KVH):
        gq_copy(g).wait()
        normed_copy(g).wait()


def write_out(*refs):
    count = len(refs) // 3
    sources, targets, held = refs[:count], refs[count : 2 * count], refs[2 * count : 3 * count]
    in_sem, out_sem = refs[3 * count :]
    reads = [pltpu.make_async_copy(sources[i], held[i], in_sem.at[i]) for i in range(count)]
    writes = [pltpu.make_async_copy(held[i], targets[i], out_sem.at[i]) for i in range(count)]
    for read in reads:
        read.start()
    for read, write in zip(reads, writes):
        read.wait()
        write.start()
    for write in writes:
        write.wait()


def local(n, pipes, replicas, q1, k1, v1, q2, k2, v2, go, gain):
    rows = q1.shape[2]
    length = n * rows
    share = QH // n
    args = [x[0, 0] for x in (q1, k1, v1, q2, k2, v2, go)] + [gain]
    anywhere = pl.BlockSpec(memory_space=pl.ANY)
    hbm = pl.BlockSpec(memory_space=pltpu.HBM)
    vmem = pl.BlockSpec(memory_space=pltpu.VMEM)
    wide = pltpu.VMEM((rows, WIDTH), BF16)
    keys = pltpu.VMEM((length, KVH * HD), BF16)
    dma = pltpu.SemaphoreType.DMA
    flops = 2 * 7 * rows * length * HD * QH
    outs = pl.pallas_call(
        functools.partial(kernel, n, pipes, replicas, rows),
        out_shape=(
            jax.ShapeDtypeStruct((rows, WIDTH), BF16),
            jax.ShapeDtypeStruct((rows, WIDTH), BF16),
            jax.ShapeDtypeStruct((rows, KVH * HD), BF16),
            jax.ShapeDtypeStruct((rows, KVH * HD), BF16),
            jax.ShapeDtypeStruct((1, WIDTH // n), F32),
        ),
        in_specs=[hbm] * 8,
        out_specs=(anywhere, anywhere, vmem, vmem, vmem),
        scratch_shapes=[
            pltpu.VMEM((1, WIDTH), BF16),
            wide, wide, wide, keys, keys, keys, keys,
            pltpu.VMEM((rows, length), F32),
            pltpu.VMEM((KVH, HPG * rows, length), F32),
            pltpu.VMEM((KVH, HPG * rows, length), BF16),
            wide, wide, wide, wide,
            pltpu.VMEM((n, KVH, 2, rows, HD), BF16),
            pltpu.VMEM((KVH, 2, length, HD), F32),
            pltpu.VMEM((n - 1, KVH, 2, rows, HD), BF16),
            pltpu.VMEM((n, share, HD), F32),
            pltpu.VMEM((n - 1, share, HD), F32),
            pltpu.VMEM((replicas, share, HD), F32),
            dma((7,)),
            dma((4, KVH, n - 1)), dma((4, KVH, n - 1)),
            dma((KVH, n - 1)), dma((KVH, n - 1)),
            dma((KVH,)),
            dma((1 + KVH,)), dma((1 + KVH,)),
            dma((n - 1,)), dma((n - 1,)),
            dma((replicas - 1,)), dma((replicas - 1,)),
        ],
        compiler_params=pltpu.CompilerParams(
            collective_id=0, has_side_effects=True, vmem_limit_bytes=VMEM_LIMIT
        ),
        cost_estimate=pl.CostEstimate(flops=flops, bytes_accessed=8 * rows * WIDTH, transcendentals=0),
    )(*args)
    nxt, gq, gk, gv, gg = pl.pallas_call(
        write_out,
        out_shape=tuple(jax.ShapeDtypeStruct(x.shape, x.dtype) for x in outs),
        in_specs=[anywhere] * 5,
        out_specs=(hbm,) * 5,
        scratch_shapes=[pltpu.VMEM(x.shape, x.dtype) for x in outs] + [dma((5,)), dma((5,))],
        compiler_params=pltpu.CompilerParams(vmem_limit_bytes=VMEM_LIMIT),
    )(*outs)
    return nxt[None, None], gq[None, None], gk[None, None], gv[None, None], gg


def solution(mesh):
    tokens = P("dp", "pipe", "seq", None)
    sizes = (mesh.shape["seq"], mesh.shape["pipe"], mesh.shape["dp"])
    return jax.shard_map(
        functools.partial(local, *sizes),
        mesh=mesh,
        in_specs=(tokens,) * 7 + (P("pipe", None),),
        out_specs=(tokens,) * 4 + (P("pipe", "seq"),),
        check_vma=False,
    )
```
